128 devices in a mesh: expert: 16 (over z, y), tensor: 8 (over x, core).
Axes of the slice: x: 4, y: 4, z: 4, core: 2. Of those that a mesh axis runs over, the one named last changes fastest.
Arguments:
- tokens: bfloat16 [4096, 4096], P('expert'), may hold values from -6 to 6
- picked: int32 [8, 16, 32], P(None, 'expert'), may hold values from 0 to 255, as said below
- counts: int32 [8, 16], replicated, may hold values from 1 to 32, 256 in all within a row
- combine: float32 [8, 16, 32], P(None, 'expert'), may hold values from 0.1 to 1
- w_in: bfloat16 [16, 4096, 4096], P('expert', None, 'tensor'), may hold values from -0.09375 to 0.09375
- w_out: bfloat16 [16, 4096, 4096], P('expert', 'tensor'), may hold values from -0.09375 to 0.09375
- w_qkv: bfloat16 [4096, 32, 3, 128], P('tensor', 'expert'), may hold values from -0.09375 to 0.09375
- upstream: bfloat16 [4096, 4096], P('expert'), may hold values from -6 to 6
Outputs:
- projected: bfloat16 [4096, 32, 3, 128], P('tensor', 'expert')
- grad_tokens: bfloat16 [4096, 4096], P('expert', 'tensor')
- grad_in: bfloat16 [16, 4096, 4096], P('expert', None, 'tensor')
- grad_out: bfloat16 [16, 4096, 4096], P('expert', 'tensor')
The draws below stay inside these ranges and needn't reach their ends.
Inputs may be any that keep to these rules, and one draw needn't show every extreme that they name: `picked`: only slots k < counts[e, s] are used; the used entries of one expert and one shard are distinct. Each expert's counts sum to 256; in every expert some shard gives exactly 32 rows.
All inputs are finite; a program needn't handle non-finite values.
Results may differ from the reference program's by a relative error of at most 0.02.
Values may be sent and summed in bfloat16 or wider, within the bound.
A program may use at most 128 MiB of HBM per device.

```python
import math
import jax
import jax.numpy as jnp
import numpy as np
from jax import lax

D = 4096
HEADS = 32
HEAD_DIM = 128
HIDDEN_SIZE = 8192
TOK_DEV = 256
ROWS_EXP = 256
EXPERTS = 8
HALF = 4096
CAP = 32
TOKENS = 4096
N_EXPERT = 16


def draw_picked(key, part):
    key = jax.random.fold_in(key, 7)
    streams = jax.random.split(key, EXPERTS * N_EXPERT)
    shuffled = jax.vmap(lambda stream: jax.random.permutation(stream, TOK_DEV)[:CAP])(streams)
    return shuffled.reshape(EXPERTS, N_EXPERT, CAP).astype(jnp.int32)


def raised(result, rng, source, target, blocks, factor):
    owner, partner = [(jnp.arange(result.shape[dim]) // (result.shape[dim] // blocks)).reshape([-1 if axis == dim else 1 for axis in range(result.ndim)]) for dim in (source, target)]
    chosen = jax.random.permutation(rng, blocks)[partner]
    strong = (owner == chosen) | (owner == (partner + blocks // 2) % blocks)
    return jnp.where(strong, factor * result, result)


def block_scale(stream_key, shape, cuts, smallest, top_value):
    factor_of = 1.0
    for dim, parts in cuts:
        draws = jax.random.uniform(jax.random.fold_in(jax.random.fold_in(stream_key, 6), dim), (parts,), jnp.float32, smallest / len(cuts), top_value / len(cuts))
        factor_of = factor_of * jnp.repeat(jnp.exp(draws), shape[dim] // parts).reshape((-1,) + (1,) * (len(shape) - 1 - dim))
    return factor_of


def length_profile(number_of, total, reach, skew):
    weights = [(1 << 20) // math.isqrt(standing ** skew) + 1 for standing in range(2, number_of + 1)]
    rest, given = total - reach - (number_of - 1), [1] * (number_of - 1)
    while rest > 0:
        free = [i for i in range(number_of - 1) if given[i] < reach]
        mass, remaining = sum([weights[i] for i in free]), rest
        for i in free:
            more = min(reach - given[i], max(1, remaining * weights[i] // mass), rest)
            given[i] = given[i] + more
            rest = rest - more
    return np.array([reach] + given)


def ragged_sizes(rng, amount, total, limit, slope):
    if amount == 2:
        one = jax.random.randint(rng, (), max(1, total - limit), min(limit, total - 1) + 1)
        return jnp.stack([one, total - one])
    sizes = jnp.asarray(length_profile(amount, total, limit, slope), jnp.int32)
    couples = (amount - 1) // 2
    giver, receiver = sizes[1:1 + 2 * couples:2], sizes[2:2 + 2 * couples:2]
    margin = jnp.minimum(giver - 1, limit - receiver)
    moved = jax.random.randint(jax.random.fold_in(rng, 1), (couples,), 0, 1 << 20) % (margin + 1)
    sizes = sizes.at[1:1 + 2 * couples:2].set(giver - moved).at[2:2 + 2 * couples:2].set(receiver + moved)
    return sizes[jax.random.permutation(jax.random.fold_in(rng, 2), amount)]


def gaussian(rng, shape, deviation, bound, cuts=(), kind=jnp.bfloat16):
    drawn = deviation * jax.random.normal(rng, shape, jnp.float32)
    if cuts:
        drawn = drawn * block_scale(rng, shape, cuts, -0.22, 0.18)
    return jnp.clip(drawn, -bound, bound).astype(kind)


def heavy_noise(key, dims, width, most, cuts, heavy, kind=jnp.bfloat16):
    result = width * jax.random.normal(key, dims, jnp.float32)
    if cuts:
        result = result * block_scale(key, dims, cuts, -0.22, 0.18)
    return jnp.clip(raised(result, jax.random.fold_in(key, 3), *heavy), -most, most).astype(kind)


def setup_inputs(seed: int = 0) -> dict:
    arg_keys = jax.random.split(jax.random.key(seed), 9)
    tokens = gaussian(arg_keys[0], (TOKENS, D), 1.0, 6.0, ((0, 16),))
    picked = draw_picked(jax.random.fold_in(arg_keys[8], 71), 0)
    counts = jax.vmap(lambda own: ragged_sizes(own, N_EXPERT, ROWS_EXP, CAP, 2))(jax.random.split(arg_keys[2], EXPERTS)).reshape((EXPERTS, N_EXPERT)).astype(jnp.int32)
    combine = jnp.clip(jnp.exp(math.log(1.0) - 2.3025851 * jax.random.uniform(arg_keys[3], (EXPERTS, N_EXPERT, CAP), jnp.float32) ** block_scale(arg_keys[3], (EXPERTS, N_EXPERT, CAP), ((1, 16),), -0.2, 0.2)), 0.1, 1.0)
    w_in = gaussian(arg_keys[4], (N_EXPERT, D, HALF), D ** -0.5, 0.09375, ((0, 16), (2, 8)))
    w_out = heavy_noise(arg_keys[5], (N_EXPERT, HALF, D), HIDDEN_SIZE ** -0.5, 0.09375, ((0, 16), (1, 8)), (1, 2, 8, 2.0))
    w_qkv = gaussian(arg_keys[6], (D, HEADS, 3, HEAD_DIM), D ** -0.5, 0.09375, ((0, 8), (1, 16)))
    upstream = gaussian(arg_keys[7], (TOKENS, D), 1.0, 6.0, ((0, 16),))
    return {"tokens": tokens, "picked": picked, "counts": counts, "combine": combine, "w_in": w_in, "w_out": w_out, "w_qkv": w_qkv, "upstream": upstream}


def gelu_value(value):
    return 0.5 * value * (1.0 + lax.erf(value * 0.7071067811865476))


def gelu_slope(value):
    return 0.5 * (1.0 + lax.erf(value * 0.7071067811865476)) + value * jnp.exp(-0.5 * value * value) * 0.3989422804014327


def rounded(value):
    return lax.optimization_barrier(value.astype(jnp.bfloat16)).astype(jnp.float32)


def reference(tokens, picked, counts, combine, w_in, w_out, w_qkv, upstream):
    slot_ids = jnp.arange(CAP, dtype=jnp.int32)
    in_use = slot_ids[None, None, :] < counts[:, :, None]
    offsets = jnp.cumsum(counts, axis=1) - counts
    position = jnp.where(in_use, offsets[:, :, None] + slot_ids[None, None, :], ROWS_EXP).astype(jnp.int32)
    owners = (picked + (jnp.arange(N_EXPERT, dtype=jnp.int32) * TOK_DEV)[None, :, None]).astype(jnp.int32)
    expert_ids = jnp.arange(EXPERTS, dtype=jnp.int32)[:, None, None] * jnp.ones_like(picked)
    owner_rows = jnp.zeros((EXPERTS, ROWS_EXP), jnp.int32).at[expert_ids, position].set(owners, mode="drop")
    weight = jnp.zeros((EXPERTS, ROWS_EXP), jnp.float32).at[expert_ids, position].set(combine, mode="drop")
    pairs_in = w_in.reshape(EXPERTS, 2, D, HALF)
    pairs_out = w_out.reshape(EXPERTS, 2, HALF, D)
    contract_last = (((1,), (1,)), ((), ()))
    contract_first = (((0,), (0,)), ((), ()))

    def one_expert(inputs):
        rows_at, scale, pair_in, pair_out = inputs
        expert_rows = tokens[rows_at]
        full_in = jnp.concatenate([pair_in[0], pair_in[1]], axis=1)
        full_out = jnp.concatenate([pair_out[0], pair_out[1]], axis=0)
        preact = jnp.dot(expert_rows, full_in, preferred_element_type=jnp.float32)
        hidden = gelu_value(preact).astype(jnp.bfloat16)
        first_half = rounded(jnp.dot(hidden[:, :HALF], pair_out[0], preferred_element_type=jnp.float32))
        second_half = rounded(jnp.dot(hidden[:, HALF:], pair_out[1], preferred_element_type=jnp.float32))
        forward = scale[:, None] * (first_half + second_half)
        row_grad = (scale[:, None] * upstream[rows_at].astype(jnp.float32)).astype(jnp.bfloat16)
        hidden_grad = lax.dot_general(row_grad, full_out, contract_last, preferred_element_type=jnp.float32)
        preact_grad = (hidden_grad * gelu_slope(preact)).astype(jnp.bfloat16)
        grad_out = lax.dot_general(hidden, row_grad, contract_first, preferred_element_type=jnp.float32).astype(jnp.bfloat16)
        grad_in = lax.dot_general(expert_rows, preact_grad, contract_first, preferred_element_type=jnp.float32).astype(jnp.bfloat16)
        back_first = rounded(lax.dot_general(preact_grad[:, :HALF], pair_in[0], contract_last, preferred_element_type=jnp.float32))
        back_second = rounded(lax.dot_general(preact_grad[:, HALF:], pair_in[1], contract_last, preferred_element_type=jnp.float32))
        grad_in_pair = jnp.stack([grad_in[:, :HALF], grad_in[:, HALF:]])
        grad_out_pair = grad_out.reshape(2, HALF, D)
        return forward, back_first + back_second, grad_in_pair, grad_out_pair

    forward, backward, grad_in, grad_out = lax.map(one_expert, (owner_rows, weight, pairs_in, pairs_out))
    flat_rows = owner_rows.reshape(-1)
    mixture = jnp.zeros((TOKENS, D), jnp.float32).at[flat_rows].add(forward.reshape(-1, D))
    layer_output = (tokens.astype(jnp.float32) + mixture).astype(jnp.bfloat16)
    projected = jnp.dot(layer_output, w_qkv.reshape(D, -1), preferred_element_type=jnp.float32)
    projected = projected.astype(jnp.bfloat16).reshape(TOKENS, HEADS, 3, HEAD_DIM)
    back_mixture = jnp.zeros((TOKENS, D), jnp.float32).at[flat_rows].add(backward.reshape(-1, D))
    grad_tokens = (upstream.astype(jnp.float32) + back_mixture).astype(jnp.bfloat16)
    return projected, grad_tokens, grad_in.reshape(N_EXPERT, D, HALF), grad_out.reshape(N_EXPERT, HALF, D)
```

```python
import jax
import jax.numpy as jnp
from jax import lax
from jax.experimental import pallas as pl
from jax.experimental.pallas import tpu as pltpu
from jax.sharding import PartitionSpec as P

BF = jnp.bfloat16
F32 = jnp.float32
NN = (((1,), (0,)), ((), ()))
NT = (((1,), (1,)), ((), ()))
TN = (((0,), (0,)), ((), ()))
RING = 4


def dot(a, b, dims=NN):
    return lax.dot_general(a, b, dims, preferred_element_type=F32)


class Wires:
    def __init__(self, send_sems, recv_sems):
        self.send_sems, self.recv_sems = send_sems, recv_sems
        self.next = 0
        self.sent = []

    def take(self, count=1):
        first = self.next
        self.next += count
        return first

    def copy(self, slot, src, dst, device):
        return pltpu.make_async_remote_copy(
            src_ref=src,
            dst_ref=dst,
            send_sem=self.send_sems.at[slot],
            recv_sem=self.recv_sems.at[slot],
            device_id=device,
            device_id_type=pl.DeviceIdType.MESH,
        )

    def send(self, slot, src, dst, device, keep=True):
        copy = self.copy(slot, src, dst, device)
        copy.start()
        if keep:
            self.sent.append(copy)

    def arrived(self, slot, dst, device):
        self.copy(slot, dst, dst, device).wait_recv()


class RingGather:
    def __init__(self, wires, at, me, minus, plus, far, to_minus, to_plus):
        self.w, self.at = wires, at
        self.me, self.minus, self.plus, self.far = me, minus, plus, far
        self.to_minus, self.to_plus = to_minus, to_plus
        self.base = wires.take(6)

    def start(self):
        b = self.base
        for i, half in enumerate((1, 0)):
            ref = self.at(self.me, half)
            self.w.send(b + i, ref, ref, self.to_plus)
            ref = self.at(self.me, 1 - half)
            self.w.send(b + 3 + i, ref, ref, self.to_minus)

    def forward(self):
        b = self.base
        ref = self.at(self.minus, 1)
        self.w.arrived(b, ref, self.to_plus)
        self.w.send(b + 2, ref, ref, self.to_plus)
        ref = self.at(self.plus, 0)
        self.w.arrived(b + 3, ref, self.to_minus)
        self.w.send(b + 5, ref, ref, self.to_minus)

    def near(self):
        self.w.arrived(self.base + 1, self.at(self.minus, 0), self.to_plus)
        self.w.arrived(self.base + 4, self.at(self.plus, 1), self.to_minus)

    def last(self):
        self.w.arrived(self.base + 2, self.at(self.far, 1), self.to_plus)
        self.w.arrived(self.base + 5, self.at(self.far, 0), self.to_minus)


def layer_kernel(
    tokens, upstream, w_in, w_out, w_qkv, picked, counts, combine,
    projected, grad_tokens, rows_out, rgrad_out, hidden_out, pgrad_out,
    tok, ups, win, wout, sel, comp, wcol,
    send_f, send_b, recv_f, recv_b, ag_f, ag_b,
    acc, slope, hid, pgr,
    pst, d2d, sbuf, half_l, half_r, full_l, full_r,
    ret_s, ret_r, lay, stage, d2dp, hl, hr, fl, fr,
    load_sems, send_sems, recv_sems,
):
    s, t = lax.axis_index("expert"), lax.axis_index("tensor")
    z, y = s // RING, s % RING
    x, c = t // 2, t % 2
    shards, experts, cap = 16, counts.shape[0], combine.shape[1]
    n_tok, width = tok.shape
    half_rows = n_tok // 2
    quarter = n_tok // 4

    def wrap(v):
        return lax.rem(v + RING, RING)

    left, right = wrap(x - 1) * 2 + c, wrap(x + 1) * 2 + c
    far = wrap(x + 2) * 2 + c
    sib = x * 2 + 1 - c
    to_left, to_right, to_sib = (s, left), (s, right), (s, sib)
    y_minus, y_plus, y_far = wrap(y - 1), wrap(y + 1), wrap(y + 2)
    z_minus, z_plus, z_far = wrap(z - 1), wrap(z + 1), wrap(z + 2)
    to_ym, to_yp = (z * RING + y_minus, t), (z * RING + y_plus, t)
    to_zm, to_zp = (z_minus * RING + y, t), (z_plus * RING + y, t)

    cols = pl.ds(pl.multiple_of(t * width, width), width)
    load_tok = pltpu.make_async_copy(tokens.at[:, cols], tok, load_sems.at[0])
    load_ups = pltpu.make_async_copy(upstream.at[:, cols], ups, load_sems.at[1])
    load_win = pltpu.make_async_copy(w_in.at[0], win, load_sems.at[2])
    load_wout = pltpu.make_async_copy(w_out.at[0], wout, load_sems.at[3])
    load_tok.start()
    load_ups.start()
    load_win.start()
    load_wout.start()

    barrier = pltpu.get_barrier_semaphore()

    def greet(i, carry):
        pl.semaphore_signal(
            barrier, inc=1, device_id=(lax.rem(s + i, shards), t),
            device_id_type=pl.DeviceIdType.MESH,
        )
        return carry

    lax.fori_loop(1, shards, greet, 0)
    for device in (to_left, to_right, to_sib):
        pl.semaphore_signal(
            barrier, inc=1, device_id=device, device_id_type=pl.DeviceIdType.MESH
        )

    slots = experts * cap
    lane = lax.broadcasted_iota(jnp.int32, (1, slots), 1)
    spread = (
        lax.broadcasted_iota(jnp.int32, (cap, slots), 1) % cap
        == lax.broadcasted_iota(jnp.int32, (cap, slots), 0)
    )
    spread = jnp.where(spread, 1.0, 0.0).astype(BF)
    wide = dot(picked[...].astype(F32).astype(BF), spread)
    own_row = (
        lax.broadcasted_iota(jnp.int32, (experts, slots), 1) // cap
        == lax.broadcasted_iota(jnp.int32, (experts, slots), 0)
    )
    pick_row = jnp.sum(jnp.where(own_row, wide, 0.0), axis=0, keepdims=True).astype(jnp.int32)
    count_row = jnp.zeros((1, slots), jnp.int32)
    for e in range(experts):
        count_row = jnp.where(lane // cap == e, counts[e, s], count_row)
    pick_row = jnp.where(lane % cap < count_row, pick_row, -1)
    token_ids = lax.broadcasted_iota(jnp.int32, (n_tok, slots), 0)
    sel[...] = jnp.where(token_ids == pick_row, 1.0, 0.0).astype(BF)

    eye = (
        lax.broadcasted_iota(jnp.int32, (cap, cap), 0)
        == lax.broadcasted_iota(jnp.int32, (cap, cap), 1)
    )
    turned = lax.dot_general(
        jnp.where(eye, 1.0, 0.0).astype(F32), combine[...], NT,
        precision=lax.Precision.HIGHEST, preferred_element_type=F32,
    )
    for e in range(experts):
        wcol[e * cap:(e + 1) * cap, :] = turned[:, e:e + 1]

    load_tok.wait()
    send_f[...] = dot(sel[...], tok[...], TN).astype(BF).reshape(send_f.shape)

    padded = shards * cap
    lane = lax.broadcasted_iota(jnp.int32, (1, padded), 1)
    mine = s // 2
    offset = jnp.int32(0)
    offset_row = jnp.zeros((1, padded), jnp.int32)
    count_row = jnp.zeros((1, padded), jnp.int32)
    for shard in range(shards):
        count = counts[mine, shard]
        here = lane // cap == shard
        offset_row = jnp.where(here, offset, offset_row)
        count_row = jnp.where(here, count, count_row)
        offset = offset + count
    position = jnp.where(lane % cap < count_row, offset_row + lane % cap, -1)
    row_ids = lax.broadcasted_iota(jnp.int32, comp.shape, 0)
    comp[...] = jnp.where(row_ids == position, 1.0, 0.0).astype(BF)

    pl.semaphore_wait(barrier, shards - 1 + 3)

    w = Wires(send_sems, recv_sems)

    def exchange(src_at, recv):
        base = w.take(shards)

        def body(i, carry):
            to = lax.rem(s + i, shards)
            w.send(base + i, src_at(to), recv.at[s], (to, t), keep=False)
            return carry

        lax.fori_loop(1, shards, body, 0)
        recv[s] = src_at(s)[...]
        return base

    def exchanged(base, recv):
        def body(i, carry):
            source = lax.rem(s - i + shards, shards)
            w.arrived(base + i, recv.at[source], (source, t))
            return carry

        lax.fori_loop(1, shards, body, 0)

    def exchange_end(base, recv):
        def body(i, carry):
            w.copy(base + i, recv.at[0], recv.at[0], to_sib).wait_send()
            return carry

        lax.fori_loop(1, shards, body, 0)

    ex_f = exchange(lambda to: send_f.at[to // 2], recv_f)

    load_ups.wait()
    taken = dot(sel[...], ups[...], TN)
    send_b[...] = (taken * wcol[...]).astype(BF).reshape(send_b.shape)
    ex_b = exchange(lambda to: send_b.at[to // 2], recv_b)

    class RowGather:
        def __init__(self, buf):
            self.buf = buf

            def at(block, half):
                return buf.at[block, pl.ds(half * half_rows, half_rows), :]

            self.ring = RingGather(w, at, t, left, right, far, to_left, to_right)
            self.base = w.take(7)
            self.at = at

        def give(self, k, ref):
            w.send(self.base + k, ref, ref, to_sib)

        def start(self):
            self.ring.start()
            self.give(0, self.buf.at[t])

        def forward(self):
            self.ring.forward()
            self.give(1, self.at(left, 1))
            self.give(2, self.at(right, 0))

        def near(self):
            self.ring.near()
            self.give(3, self.at(left, 0))
            self.give(4, self.at(right, 1))

        def last(self):
            self.ring.last()
            self.give(5, self.at(far, 1))
            self.give(6, self.at(far, 0))

        def sib_own(self):
            w.arrived(self.base, self.buf.at[sib], to_sib)

        def sib_near(self):
            other = 1 - 2 * c
            for k, (block, half) in enumerate(((left, 1), (right, 0), (left, 0), (right, 1))):
                w.arrived(self.base + 1 + k, self.at(block + other, half), to_sib)

        def sib_last(self):
            other = 1 - 2 * c
            w.arrived(self.base + 5, self.at(far + other, 1), to_sib)
            w.arrived(self.base + 6, self.at(far + other, 0), to_sib)

    other = 1 - 2 * c

    def win_at(j):
        return win[pl.ds(pl.multiple_of(j * width, width), width), :]

    def wout_at(j):
        return wout[:, pl.ds(pl.multiple_of(j * width, width), width)]

    def gathered(gather, weight_at, dims):
        buf = gather.buf

        def add(j, first=False):
            term = dot(buf[j], weight_at(j), dims)
            if first:
                acc[...] = term
            else:
                acc[...] += term

        add(t, True)
        gather.sib_own()
        add(sib)
        gather.near()
        add(left)
        add(right)
        gather.last()
        gather.sib_near()
        add(left + other)
        add(right + other)
        add(far)
        gather.sib_last()
        add(far + other)

    class RowReduce:
        def __init__(self, k):
            self.k = k
            self.base = w.take(10)

        def partials(self, lhs, weight_at, dims):
            k, b = self.k, self.base
            for d in (2, 1, 3, 0):
                j = wrap(x + d) * 2 + 1 - c
                pst[k, d] = dot(lhs[...], weight_at(j), dims).astype(BF)
                w.send(b + d, pst.at[k, d], d2d.at[k, d], to_sib)
            lo, hi = pl.ds(0, half_rows), pl.ds(half_rows, half_rows)
            for d in (2, 1, 3, 0):
                j = wrap(x + d) * 2 + c
                own = dot(lhs[...], weight_at(j), dims)
                w.arrived(b + d, d2d.at[k, d], to_sib)
                sbuf[k, d] = (own + d2d[k, d].astype(F32)).astype(BF)
                if d == 2:
                    w.send(b + 4, sbuf.at[k, d, hi], half_l.at[k], to_right)
                    w.send(b + 5, sbuf.at[k, d, lo], half_r.at[k], to_left)
                elif d == 1:
                    w.send(b + 6, sbuf.at[k, d, lo], full_l.at[k, lo], to_right)
                elif d == 3:
                    w.send(b + 7, sbuf.at[k, d, hi], full_r.at[k, hi], to_left)

        def forward(self):
            k, b = self.k, self.base
            lo, hi = pl.ds(0, half_rows), pl.ds(half_rows, half_rows)
            w.arrived(b + 4, half_l.at[k], to_right)
            sbuf[k, 1, hi] = (sbuf[k, 1, hi].astype(F32) + half_l[k].astype(F32)).astype(BF)
            w.send(b + 8, sbuf.at[k, 1, hi], full_l.at[k, hi], to_right)
            w.arrived(b + 5, half_r.at[k], to_left)
            sbuf[k, 3, lo] = (sbuf[k, 3, lo].astype(F32) + half_r[k].astype(F32)).astype(BF)
            w.send(b + 9, sbuf.at[k, 3, lo], full_r.at[k, lo], to_left)

        def result(self):
            k, b = self.k, self.base
            lo, hi = pl.ds(0, half_rows), pl.ds(half_rows, half_rows)
            w.arrived(b + 6, full_l.at[k, lo], to_right)
            w.arrived(b + 7, full_r.at[k, hi], to_left)
            w.arrived(b + 8, full_l.at[k, hi], to_right)
            w.arrived(b + 9, full_r.at[k, lo], to_left)
            total = sbuf[k, 0].astype(F32) + full_l[k].astype(F32) + full_r[k].astype(F32)
            return total.astype(BF)

    def send_back(k, rows):
        ret_s[k] = dot(comp[...], rows, TN).astype(BF).reshape(ret_s.shape[1:])
        return exchange(lambda to: ret_s.at[k, to], ret_r.at[k])

    def returned(k, base):
        exchanged(base, ret_r.at[k])
        pairs = ret_r[k].reshape(experts, 2, cap, width).astype(F32)
        return (pairs[:, 0] + pairs[:, 1]).reshape(slots, width)

    def scatter(values):
        high = values.astype(BF)
        low = (values - high.astype(F32)).astype(BF)
        return dot(sel[...], high) + dot(sel[...], low)

    gather_f = RowGather(ag_f)
    gather_b = RowGather(ag_b)
    exchanged(ex_f, recv_f)
    ag_f[t] = dot(comp[...], recv_f[...].reshape(padded, width)).astype(BF)
    gather_f.start()
    gather_f.forward()
    load_win.wait()
    gathered(gather_f, win_at, NN)
    pre = acc[...]
    cdf = 0.5 * (1.0 + lax.erf(pre * 0.7071067811865476))
    hid[...] = (pre * cdf).astype(BF)
    slope[...] = cdf + pre * jnp.exp(-0.5 * pre * pre) * 0.3989422804014327
    load_wout.wait()
    reduce_f = RowReduce(0)
    reduce_f.partials(hid, wout_at, NN)

    save_rows = pltpu.make_async_copy(ag_f, rows_out, load_sems.at[0])
    save_rows.start()
    save_hid = pltpu.make_async_copy(hid, hidden_out, load_sems.at[1])
    save_hid.start()

    exchanged(ex_b, recv_b)
    ag_b[t] = dot(comp[...], recv_b[...].reshape(padded, width)).astype(BF)
    reduce_f.forward()
    gather_b.start()
    back_f = send_back(0, reduce_f.result())
    gather_b.forward()

    halves = returned(0, back_f)
    mixture = scatter(halves * wcol[...])
    lay[s] = (tok[...].astype(F32) + mixture).astype(BF)

    def lay_at(part, along_z, fixed):
        def at(pos, half):
            index = pos * RING + fixed if along_z else fixed + pos
            return lay.at[index, pl.ds(part * half_rows + half * quarter, quarter), :]
        return at

    def along_y(part, zz):
        return RingGather(
            w, lay_at(part, False, zz * RING), y, y_minus, y_plus, y_far, to_ym, to_yp
        )

    def along_z(part, yy):
        return RingGather(
            w, lay_at(part, True, yy), z, z_minus, z_plus, z_far, to_zm, to_zp
        )

    first_p, first_q = along_y(0, z), along_z(1, y)
    second_p = [along_z(0, yy) for yy in (y, y_minus, y_plus, y_far)]
    second_q = [along_y(1, zz) for zz in (z, z_minus, z_plus, z_far)]
    first_p.start()
    first_q.start()
    second_p[0].start()
    second_q[0].start()

    first_p.forward()
    first_q.forward()
    gathered(gather_b, wout_at, NT)
    pgr[...] = (acc[...] * slope[...]).astype(BF)
    save_rgrad = pltpu.make_async_copy(ag_b, rgrad_out, load_sems.at[2])
    save_rgrad.start()
    save_pgr = pltpu.make_async_copy(pgr, pgrad_out, load_sems.at[3])
    save_pgr.start()

    first_p.near()
    first_q.near()
    for k in (1, 2):
        second_p[k].start()
        second_q[k].start()
    first_p.last()
    first_q.last()
    second_p[3].start()
    second_q[3].start()
    second_p[0].forward()
    second_q[0].forward()

    reduce_b = RowReduce(1)
    reduce_b.partials(pgr, win_at, NT)

    for k in (1, 2):
        second_p[k].forward()
        second_q[k].forward()

    unit_base = w.take(8)
    x_base = w.take(12)

    def unit(q, zp, cp):
        for i in range(2):
            block = lay[zp * RING + cp * 2 + i, q * half_rows:(q + 1) * half_rows, :]
            stage[q, cp, zp, i * half_rows:(i + 1) * half_rows, :] = dot(
                block, w_qkv[...]
            ).astype(BF)

        @pl.when(cp != c)
        def _():
            w.send(
                unit_base + q * RING + zp, stage.at[q, cp, zp], d2dp.at[q, zp], to_sib,
                keep=False,
            )

    lo, hi = pl.ds(0, half_rows), pl.ds(half_rows, half_rows)

    def settle(q, zp):
        b = x_base + q * 6
        w.arrived(unit_base + q * RING + zp, d2dp.at[q, zp], to_sib)
        stage[q, c, zp] = (
            stage[q, c, zp].astype(F32) + d2dp[q, zp].astype(F32)
        ).astype(BF)
        d = wrap(zp - x)

        @pl.when(d == 2)
        def _():
            w.send(b, stage.at[q, c, zp, hi], hl.at[q], to_right, keep=False)
            w.send(b + 1, stage.at[q, c, zp, lo], hr.at[q], to_left, keep=False)

        @pl.when(d == 1)
        def _():
            w.send(b + 2, stage.at[q, c, zp, lo], fl.at[q, lo], to_right, keep=False)

        @pl.when(d == 3)
        def _():
            w.send(b + 3, stage.at[q, c, zp, hi], fr.at[q, hi], to_left, keep=False)

    def pass_on(q):
        b = x_base + q * 6
        zr, zl = wrap(x + 1), wrap(x - 1)
        w.arrived(b, hl.at[q], to_right)
        stage[q, c, zr, hi] = (
            stage[q, c, zr, hi].astype(F32) + hl[q].astype(F32)
        ).astype(BF)
        w.send(b + 4, stage.at[q, c, zr, hi], fl.at[q, hi], to_right, keep=False)
        w.arrived(b + 1, hr.at[q], to_left)
        stage[q, c, zl, lo] = (
            stage[q, c, zl, lo].astype(F32) + hr[q].astype(F32)
        ).astype(BF)
        w.send(b + 5, stage.at[q, c, zl, lo], fr.at[q, lo], to_left, keep=False)

    def finish(q):
        b = x_base + q * 6
        w.arrived(b + 2, fl.at[q, lo], to_right)
        w.arrived(b + 3, fr.at[q, hi], to_left)
        w.arrived(b + 4, fl.at[q, hi], to_right)
        w.arrived(b + 5, fr.at[q, lo], to_left)
        total = (
            stage[q, c, x].astype(F32) + fl[q].astype(F32) + fr[q].astype(F32)
        ).astype(BF)
        for i in range(2):
            first = i * n_tok + q * half_rows
            projected[first:first + half_rows, :] = total[i * half_rows:(i + 1) * half_rows]

    z_order = (z, z_plus, z_minus, z_far)
    pair = y // 2

    unit(0, z, 0)
    unit(0, z, 1)
    reduce_b.forward()
    for k in range(4):
        second_q[k].near()
    second_p[3].forward()
    second_q[3].forward()
    for zp in z_order:
        unit(1, zp, pair)
    settle(0, z)
    back_b = send_back(1, reduce_b.result())
    for k in range(4):
        second_p[k].near()
    for zp in (z_plus, z_minus):
        unit(0, zp, 0)
        unit(0, zp, 1)

    @pl.when(pair == c)
    def _():
        for zp in z_order:
            settle(1, zp)

    for k in range(4):
        second_p[k].last()
    unit(0, z_far, 0)
    unit(0, z_far, 1)
    for zp in (z_plus, z_minus, z_far):
        settle(0, zp)
    for k in range(4):
        second_q[k].last()
    for zp in z_order:
        unit(1, zp, 1 - pair)
    pass_on(0)

    @pl.when(pair != c)
    def _():
        for zp in z_order:
            settle(1, zp)

    back_rows = scatter(returned(1, back_b))
    grad_tokens[...] = (ups[...].astype(F32) + back_rows).astype(BF)
    pass_on(1)
    finish(0)
    finish(1)

    for copy in w.sent:
        copy.wait_send()
    exchange_end(ex_f, recv_f)
    exchange_end(ex_b, recv_b)
    exchange_end(back_f, ret_r.at[0])
    exchange_end(back_b, ret_r.at[1])

    for q in range(2):
        for k in range(RING):
            w.copy(unit_base + q * RING + k, d2dp.at[q, k], d2dp.at[q, k], to_sib).wait_send()
        for k in range(6):
            w.copy(x_base + q * 6 + k, hl.at[q], hl.at[q], to_left).wait_send()
    save_rows.wait()
    save_hid.wait()
    save_rgrad.wait()
    save_pgr.wait()


def weight_grad_kernel(rows, rgrad, hidden, pgrad, grad_in, grad_out):
    grad_in[0] = dot(rows[0], pgrad[...], TN).astype(BF)
    grad_out[0] = dot(hidden[...], rgrad[0], TN).astype(BF)


def on_device(tokens, picked, counts, combine, w_in, w_out, w_qkv, upstream):
    n_tok, width = tokens.shape
    experts, cap = picked.shape[0], picked.shape[2]
    parts, shards = 8, 16
    slice_w = width // parts
    rows = experts * cap
    hidden = w_in.shape[2]
    flat = w_qkv.reshape(slice_w, -1)
    columns = flat.shape[1]
    half = n_tok // 2
    anywhere = pl.BlockSpec(memory_space=pl.ANY)
    vmem = pl.BlockSpec(memory_space=pltpu.VMEM)
    smem = pl.BlockSpec(memory_space=pltpu.SMEM)
    sems = 340
    out = pl.pallas_call(
        layer_kernel,
        out_shape=(
            jax.ShapeDtypeStruct((2 * n_tok, columns), BF),
            jax.ShapeDtypeStruct((n_tok, slice_w), BF),
            jax.ShapeDtypeStruct((parts, rows, slice_w), BF),
            jax.ShapeDtypeStruct((parts, rows, slice_w), BF),
            jax.ShapeDtypeStruct((rows, hidden), BF),
            jax.ShapeDtypeStruct((rows, hidden), BF),
        ),
        in_specs=[anywhere] * 4 + [vmem, vmem, smem, vmem],
        out_specs=[vmem, vmem] + [anywhere] * 4,
        scratch_shapes=[
            pltpu.VMEM((n_tok, slice_w), BF),
            pltpu.VMEM((n_tok, slice_w), BF),
            pltpu.VMEM((width, hidden), BF),
            pltpu.VMEM((hidden, width), BF),
            pltpu.VMEM((n_tok, rows), BF),
            pltpu.VMEM((rows, shards * cap), BF),
            pltpu.VMEM((rows, 1), F32),
            pltpu.VMEM((experts, cap, slice_w), BF),
            pltpu.VMEM((experts, cap, slice_w), BF),
            pltpu.VMEM((shards, cap, slice_w), BF),
            pltpu.VMEM((shards, cap, slice_w), BF),
            pltpu.VMEM((parts, rows, slice_w), BF),
            pltpu.VMEM((parts, rows, slice_w), BF),
            pltpu.VMEM((rows, hidden), F32),
            pltpu.VMEM((rows, hidden), F32),
            pltpu.VMEM((rows, hidden), BF),
            pltpu.VMEM((rows, hidden), BF),
            pltpu.VMEM((2, RING, rows, slice_w), BF),
            pltpu.VMEM((2, RING, rows, slice_w), BF),
            pltpu.VMEM((2, RING, rows, slice_w), BF),
            pltpu.VMEM((2, rows // 2, slice_w), BF),
            pltpu.VMEM((2, rows // 2, slice_w), BF),
            pltpu.VMEM((2, rows, slice_w), BF),
            pltpu.VMEM((2, rows, slice_w), BF),
            pltpu.VMEM((2, shards, cap, slice_w), BF),
            pltpu.VMEM((2, shards, cap, slice_w), BF),
            pltpu.VMEM((shards, n_tok, slice_w), BF),
            pltpu.VMEM((2, 2, RING, n_tok, columns), BF),
            pltpu.VMEM((2, RING, n_tok, columns), BF),
            pltpu.VMEM((2, half, columns), BF),
            pltpu.VMEM((2, half, columns), BF),
            pltpu.VMEM((2, n_tok, columns), BF),
            pltpu.VMEM((2, n_tok, columns), BF),
            pltpu.SemaphoreType.DMA((4,)),
            pltpu.SemaphoreType.DMA((sems,)),
            pltpu.SemaphoreType.DMA((sems,)),
        ],
        compiler_params=pltpu.CompilerParams(
            collective_id=0, has_side_effects=True, vmem_limit_bytes=62 * 1024 * 1024
        ),
        cost_estimate=pl.CostEstimate(
            flops=8 * 10**9, bytes_accessed=20 * 10**6, transcendentals=3 * 10**5
        ),
        name="moe_layer",
    )(
        tokens, upstream, w_in, w_out, flat,
        picked[:, 0, :], counts, combine[:, 0, :],
    )
    projected, grad_tokens, taken, row_grad, hid, preact_grad = out
    whole = lambda shape: pl.BlockSpec(shape, lambda j: (0, 0))
    grad_in, grad_out = pl.pallas_call(
        weight_grad_kernel,
        grid=(parts,),
        out_shape=(
            jax.ShapeDtypeStruct(w_in.shape, BF),
            jax.ShapeDtypeStruct(w_out.shape, BF),
        ),
        in_specs=[
            pl.BlockSpec((1, rows, slice_w), lambda j: (j, 0, 0)),
            pl.BlockSpec((1, rows, slice_w), lambda j: (j, 0, 0)),
            whole((rows, hidden)),
            whole((rows, hidden)),
        ],
        out_specs=(
            pl.BlockSpec((1, slice_w, hidden), lambda j: (0, j, 0)),
            pl.BlockSpec((1, hidden, slice_w), lambda j: (0, 0, j)),
        ),
        compiler_params=pltpu.CompilerParams(vmem_limit_bytes=32 * 1024 * 1024),
        cost_estimate=pl.CostEstimate(
            flops=2 * 10**9, bytes_accessed=12 * 10**6, transcendentals=0
        ),
        name="weight_grads",
    )(taken, row_grad, hid, preact_grad)
    return (projected.reshape(2 * n_tok, *w_qkv.shape[1:]), grad_tokens, grad_in, grad_out)


def solution(mesh):
    return jax.shard_map(
        on_device,
        mesh=mesh,
        in_specs=(
            P("expert", None),
            P(None, "expert", None),
            P(),
            P(None, "expert", None),
            P("expert", None, "tensor"),
            P("expert", "tensor", None),
            P("tensor", "expert", None, None),
            P("expert", None),
        ),
        out_specs=(
            P("tensor", "expert", None, None),
            P("expert", "tensor"),
            P("expert", None, "tensor"),
            P("expert", "tensor", None),
        ),
        check_vma=False,
    )
```

```python
import jax
import jax.numpy as jnp
from jax import lax
from jax.experimental import pallas as pl
from jax.experimental.pallas import tpu as pltpu
from jax.sharding import PartitionSpec as P

BF = jnp.bfloat16
F32 = jnp.float32
NN = (((1,), (0,)), ((), ()))
NT = (((1,), (1,)), ((), ()))
TN = (((0,), (0,)), ((), ()))
RING = 4
BAND = 32


def dot(a, b, dims=NN):
    return lax.dot_general(a, b, dims, preferred_element_type=F32)


def row_permutation(blocks, gather):
    n = BAND * blocks
    a = lax.broadcasted_iota(jnp.int32, (n, n), 0)
    b = lax.broadcasted_iota(jnp.int32, (n, n), 1)
    if not gather:
        a, b = b, a
    return jnp.where((a % BAND) * blocks + a // BAND == b, 1.0, 0.0).astype(BF)


class Wires:
    def __init__(self, send_sems, recv_sems):
        self.send_sems, self.recv_sems = send_sems, recv_sems
        self.next = 0
        self.sent = []

    def take(self, count=1):
        first = self.next
        self.next += count
        return first

    def copy(self, slot, src, dst, device):
        return pltpu.make_async_remote_copy(
            src_ref=src,
            dst_ref=dst,
            send_sem=self.send_sems.at[slot],
            recv_sem=self.recv_sems.at[slot],
            device_id=device,
            device_id_type=pl.DeviceIdType.MESH,
        )

    def send(self, slot, src, dst, device, keep=True):
        copy = self.copy(slot, src, dst, device)
        copy.start()
        if keep:
            self.sent.append(copy)

    def arrived(self, slot, dst, device):
        self.copy(slot, dst, dst, device).wait_recv()


class RingGather:
    def __init__(self, wires, at, me, minus, plus, far, to_minus, to_plus):
        self.w, self.at = wires, at
        self.me, self.minus, self.plus, self.far = me, minus, plus, far
        self.to_minus, self.to_plus = to_minus, to_plus
        self.base = wires.take(6)

    def start(self):
        b = self.base
        for i, half in enumerate((1, 0)):
            ref = self.at(self.me, half)
            self.w.send(b + i, ref, ref, self.to_plus)
            ref = self.at(self.me, 1 - half)
            self.w.send(b + 3 + i, ref, ref, self.to_minus)

    def forward(self):
        b = self.base
        ref = self.at(self.minus, 1)
        self.w.arrived(b, ref, self.to_plus)
        self.w.send(b + 2, ref, ref, self.to_plus)
        ref = self.at(self.plus, 0)
        self.w.arrived(b + 3, ref, self.to_minus)
        self.w.send(b + 5, ref, ref, self.to_minus)

    def near(self):
        self.w.arrived(self.base + 1, self.at(self.minus, 0), self.to_plus)
        self.w.arrived(self.base + 4, self.at(self.plus, 1), self.to_minus)

    def last(self):
        self.w.arrived(self.base + 2, self.at(self.far, 1), self.to_plus)
        self.w.arrived(self.base + 5, self.at(self.far, 0), self.to_minus)


def layer_kernel(
    tokens, upstream, w_in, w_out, w_qkv, picked, counts, combine,
    projected, grad_tokens, rows_out, rgrad_out, hidden_out, pgrad_out,
    tok, ups, ups_half, win, wout, wraw, wqkv, sel, comp, wcol,
    send_f, send_b, recv_f, recv_b, ag_f, ag_b,
    acc, slope, hid, pgr,
    pst, d2d, sbuf, half_l, half_r, full_l, full_r,
    ret_s, ret_r, lay, stage, d2dp, hl, hr, fl, fr,
    load_sems, send_sems, recv_sems,
):
    s, t = lax.axis_index("expert"), lax.axis_index("tensor")
    z, y = s // RING, s % RING
    x, c = t // 2, t % 2
    shards, experts, cap = 16, counts.shape[0], combine.shape[1]
    n_tok, width = tok.shape
    half_rows = n_tok // 2
    quarter = n_tok // 4

    def wrap(v):
        return lax.rem(v + RING, RING)

    left, right = wrap(x - 1) * 2 + c, wrap(x + 1) * 2 + c
    far = wrap(x + 2) * 2 + c
    sib = x * 2 + 1 - c
    to_left, to_right, to_sib = (s, left), (s, right), (s, sib)
    y_minus, y_plus, y_far = wrap(y - 1), wrap(y + 1), wrap(y + 2)
    z_minus, z_plus, z_far = wrap(z - 1), wrap(z + 1), wrap(z + 2)
    to_ym, to_yp = (z * RING + y_minus, t), (z * RING + y_plus, t)
    to_zm, to_zp = (z_minus * RING + y, t), (z_plus * RING + y, t)

    cols = pl.ds(pl.multiple_of(t * width, width), width)
    load_tok = pltpu.make_async_copy(tokens.at[:, cols], tok, load_sems.at[0])
    load_ups = pltpu.make_async_copy(upstream.at[:, cols], ups, load_sems.at[1])
    load_win = pltpu.make_async_copy(w_in.at[0], win, load_sems.at[2])
    load_wout = pltpu.make_async_copy(w_out.at[0], wout, load_sems.at[3])
    wide_cols = pl.ds(pl.multiple_of(c * RING * width, width), RING * width)
    load_half = pltpu.make_async_copy(upstream.at[:, wide_cols], ups_half, load_sems.at[4])
    load_qkv = pltpu.make_async_copy(w_qkv, wraw, load_sems.at[5])
    load_tok.start()
    load_half.start()
    load_win.start()
    load_wout.start()
    load_qkv.start()
    load_ups.start()

    barrier = pltpu.get_barrier_semaphore()

    def greet(i, carry):
        pl.semaphore_signal(
            barrier, inc=1, device_id=(lax.rem(s + i, shards), t),
            device_id_type=pl.DeviceIdType.MESH,
        )
        return carry

    lax.fori_loop(1, shards, greet, 0)
    for device in (to_left, to_right, to_sib):
        pl.semaphore_signal(
            barrier, inc=1, device_id=device, device_id_type=pl.DeviceIdType.MESH
        )

    slots = experts * cap
    lane = lax.broadcasted_iota(jnp.int32, (1, slots), 1)
    spread = (
        lax.broadcasted_iota(jnp.int32, (cap, slots), 1) % cap
        == lax.broadcasted_iota(jnp.int32, (cap, slots), 0)
    )
    spread = jnp.where(spread, 1.0, 0.0).astype(BF)
    wide = dot(picked[...].astype(F32).astype(BF), spread)
    own_row = (
        lax.broadcasted_iota(jnp.int32, (experts, slots), 1) // cap
        == lax.broadcasted_iota(jnp.int32, (experts, slots), 0)
    )
    pick_row = jnp.sum(jnp.where(own_row, wide, 0.0), axis=0, keepdims=True).astype(jnp.int32)
    count_row = jnp.zeros((1, slots), jnp.int32)
    for e in range(experts):
        count_row = jnp.where(lane // cap == e, counts[e, s], count_row)
    pick_row = jnp.where(lane % cap < count_row, pick_row, -1)
    token_ids = lax.broadcasted_iota(jnp.int32, (n_tok, slots), 0)
    sel[...] = jnp.where(token_ids == pick_row, 1.0, 0.0).astype(BF)

    load_tok.wait()
    send_f[...] = dot(sel[...], tok[...], TN).astype(BF).reshape(send_f.shape)

    pl.semaphore_wait(barrier, shards - 1 + 3)

    w = Wires(send_sems, recv_sems)

    def exchange(src_at, recv):
        base = w.take(shards)

        def body(i, carry):
            to = lax.rem(s + i, shards)
            w.send(base + i, src_at(to), recv.at[s], (to, t), keep=False)
            return carry

        lax.fori_loop(1, shards, body, 0)
        recv[s] = src_at(s)[...]
        return base

    def exchanged(base, recv):
        def body(i, carry):
            source = lax.rem(s - i + shards, shards)
            w.arrived(base + i, recv.at[source], (source, t))
            return carry

        lax.fori_loop(1, shards, body, 0)

    def exchange_end(base, recv):
        def body(i, carry):
            w.copy(base + i, recv.at[0], recv.at[0], to_sib).wait_send()
            return carry

        lax.fori_loop(1, shards, body, 0)

    ex_f = exchange(lambda to: send_f.at[to // 2], recv_f)

    eye = (
        lax.broadcasted_iota(jnp.int32, (cap, cap), 0)
        == lax.broadcasted_iota(jnp.int32, (cap, cap), 1)
    )
    turned = lax.dot_general(
        jnp.where(eye, 1.0, 0.0).astype(F32), combine[...], NT,
        precision=lax.Precision.HIGHEST, preferred_element_type=F32,
    )
    for e in range(experts):
        wcol[e * cap:(e + 1) * cap, :] = turned[:, e:e + 1]

    padded = shards * cap
    lane = lax.broadcasted_iota(jnp.int32, (1, padded), 1)
    mine = s // 2
    offset = jnp.int32(0)
    offset_row = jnp.zeros((1, padded), jnp.int32)
    count_row = jnp.zeros((1, padded), jnp.int32)
    for shard in range(shards):
        count = counts[mine, shard]
        here = lane // cap == shard
        offset_row = jnp.where(here, offset, offset_row)
        count_row = jnp.where(here, count, count_row)
        offset = offset + count
    position = jnp.where(lane % cap < count_row, offset_row + lane % cap, -1)
    row_ids = lax.broadcasted_iota(jnp.int32, comp.shape, 0)
    comp[...] = jnp.where(row_ids == position, 1.0, 0.0).astype(BF)

    load_half.wait()
    for k in range(RING):
        part = slice(k * width, (k + 1) * width)
        taken = dot(sel[...], ups_half[:, part], TN) * wcol[...]
        send_b[:, :, part] = taken.astype(BF).reshape(experts, cap, width)

    load_qkv.wait()
    blocks = wqkv.shape[1] // 128
    turn = row_permutation(blocks, True)
    for f in range(0, width, BAND):
        moved = dot(turn, wraw[f * blocks:(f + BAND) * blocks, :]).astype(BF)
        for k in range(blocks):
            wqkv[f:f + BAND, k * 128:(k + 1) * 128] = moved[k * BAND:(k + 1) * BAND]

    class RowGather:
        def __init__(self, buf):
            self.buf = buf

            def at(block, half):
                return buf.at[block, pl.ds(half * half_rows, half_rows), :]

            self.ring = RingGather(w, at, t, left, right, far, to_left, to_right)
            self.base = w.take(7)
            self.at = at

        def give(self, k, ref):
            w.send(self.base + k, ref, ref, to_sib)

        def start(self):
            self.ring.start()
            self.give(0, self.buf.at[t])

        def forward(self):
            self.ring.forward()
            self.give(1, self.at(left, 1))
            self.give(2, self.at(right, 0))

        def near(self):
            self.ring.near()
            self.give(3, self.at(left, 0))
            self.give(4, self.at(right, 1))

        def last(self):
            self.ring.last()
            self.give(5, self.at(far, 1))
            self.give(6, self.at(far, 0))

        def sib_own(self):
            w.arrived(self.base, self.buf.at[sib], to_sib)

        def sib_near(self):
            other = 1 - 2 * c
            for k, (block, half) in enumerate(((left, 1), (right, 0), (left, 0), (right, 1))):
                w.arrived(self.base + 1 + k, self.at(block + other, half), to_sib)

        def sib_last(self):
            other = 1 - 2 * c
            w.arrived(self.base + 5, self.at(far + other, 1), to_sib)
            w.arrived(self.base + 6, self.at(far + other, 0), to_sib)

    other = 1 - 2 * c

    def win_at(j):
        return win[pl.ds(pl.multiple_of(j * width, width), width), :]

    def wout_at(j):
        return wout[:, pl.ds(pl.multiple_of(j * width, width), width)]

    def gathered(gather, weight_at, dims):
        buf = gather.buf

        def add(j, first=False):
            term = dot(buf[j], weight_at(j), dims)
            if first:
                acc[...] = term
            else:
                acc[...] += term

        add(t, True)
        gather.sib_own()
        add(sib)
        gather.near()
        add(left)
        add(right)
        gather.last()
        gather.sib_near()
        add(left + other)
        add(right + other)
        add(far)
        gather.sib_last()
        add(far + other)

    class RowReduce:
        def __init__(self, k):
            self.k = k
            self.base = w.take(10)

        def partials(self, lhs, weight_at, dims):
            k, b = self.k, self.base
            for d in (2, 1, 3, 0):
                j = wrap(x + d) * 2 + 1 - c
                pst[k, d] = dot(lhs[...], weight_at(j), dims).astype(BF)
                w.send(b + d, pst.at[k, d], d2d.at[k, d], to_sib)
            lo, hi = pl.ds(0, half_rows), pl.ds(half_rows, half_rows)
            for d in (2, 1, 3, 0):
                j = wrap(x + d) * 2 + c
                own = dot(lhs[...], weight_at(j), dims)
                w.arrived(b + d, d2d.at[k, d], to_sib)
                sbuf[k, d] = (own + d2d[k, d].astype(F32)).astype(BF)
                if d == 2:
                    w.send(b + 4, sbuf.at[k, d, hi], half_l.at[k], to_right)
                    w.send(b + 5, sbuf.at[k, d, lo], half_r.at[k], to_left)
                elif d == 1:
                    w.send(b + 6, sbuf.at[k, d, lo], full_l.at[k, lo], to_right)
                elif d == 3:
                    w.send(b + 7, sbuf.at[k, d, hi], full_r.at[k, hi], to_left)

        def forward(self):
            k, b = self.k, self.base
            lo, hi = pl.ds(0, half_rows), pl.ds(half_rows, half_rows)
            w.arrived(b + 4, half_l.at[k], to_right)
            sbuf[k, 1, hi] = (sbuf[k, 1, hi].astype(F32) + half_l[k].astype(F32)).astype(BF)
            w.send(b + 8, sbuf.at[k, 1, hi], full_l.at[k, hi], to_right)
            w.arrived(b + 5, half_r.at[k], to_left)
            sbuf[k, 3, lo] = (sbuf[k, 3, lo].astype(F32) + half_r[k].astype(F32)).astype(BF)
            w.send(b + 9, sbuf.at[k, 3, lo], full_r.at[k, lo], to_left)

        def result(self):
            k, b = self.k, self.base
            lo, hi = pl.ds(0, half_rows), pl.ds(half_rows, half_rows)
            w.arrived(b + 6, full_l.at[k, lo], to_right)
            w.arrived(b + 7, full_r.at[k, hi], to_left)
            w.arrived(b + 8, full_l.at[k, hi], to_right)
            w.arrived(b + 9, full_r.at[k, lo], to_left)
            total = sbuf[k, 0].astype(F32) + full_l[k].astype(F32) + full_r[k].astype(F32)
            return total.astype(BF)

    def send_back(k, rows):
        ret_s[k] = dot(comp[...], rows, TN).astype(BF).reshape(ret_s.shape[1:])
        return exchange(lambda to: ret_s.at[k, to], ret_r.at[k])

    def returned(k, base):
        exchanged(base, ret_r.at[k])
        pairs = ret_r[k].reshape(experts, 2, cap, width).astype(F32)
        return (pairs[:, 0] + pairs[:, 1]).reshape(slots, width)

    def scatter(values):
        high = values.astype(BF)
        low = (values - high.astype(F32)).astype(BF)
        return dot(sel[...], high) + dot(sel[...], low)

    gather_f = RowGather(ag_f)
    exchanged(ex_f, recv_f)
    ag_f[t] = dot(comp[...], recv_f[...].reshape(padded, width)).astype(BF)
    gather_f.start()
    ex_b = exchange(lambda to: send_b.at[to // 2], recv_b)
    gather_f.forward()
    load_win.wait()
    gathered(gather_f, win_at, NN)
    pre = acc[...]
    cdf = 0.5 * (1.0 + lax.erf(pre * 0.7071067811865476))
    hid[...] = (pre * cdf).astype(BF)
    slope[...] = cdf + pre * jnp.exp(-0.5 * pre * pre) * 0.3989422804014327
    load_wout.wait()
    reduce_f = RowReduce(0)
    reduce_f.partials(hid, wout_at, NN)

    save_rows = pltpu.make_async_copy(ag_f, rows_out, load_sems.at[6])
    save_rows.start()
    save_hid = pltpu.make_async_copy(hid, hidden_out, load_sems.at[7])
    save_hid.start()

    reduce_f.forward()
    back_f = send_back(0, reduce_f.result())

    give_b = w.take(RING)
    exchanged(ex_b, recv_b)
    for k in range(RING):
        part = recv_b[:, :, k * width:(k + 1) * width].reshape(padded, width)
        mine_k = ag_b.at[c * RING + k]
        mine_k[...] = dot(comp[...], part).astype(BF)
        w.send(give_b + k, mine_k, mine_k, to_sib)
    for k in range(2 * RING):
        j = c * RING + k if k < RING else (1 - c) * RING + k - RING
        if k >= RING:
            w.arrived(give_b + k - RING, ag_b.at[j], to_sib)
        term = dot(ag_b[j], wout_at(j), NT)
        if k == 0:
            acc[...] = term
        else:
            acc[...] += term
    pgr[...] = (acc[...] * slope[...]).astype(BF)
    save_rgrad = pltpu.make_async_copy(ag_b, rgrad_out, load_sems.at[8])
    save_rgrad.start()
    save_pgr = pltpu.make_async_copy(pgr, pgrad_out, load_sems.at[9])
    save_pgr.start()
    reduce_b = RowReduce(1)
    reduce_b.partials(pgr, win_at, NT)

    halves = returned(0, back_f)
    mixture = scatter(halves * wcol[...])
    lay[s] = (tok[...].astype(F32) + mixture).astype(BF)

    def lay_at(part, along_z, fixed):
        def at(pos, half):
            index = pos * RING + fixed if along_z else fixed + pos
            return lay.at[index, pl.ds(part * half_rows + half * quarter, quarter), :]
        return at

    def along_y(part, zz):
        return RingGather(
            w, lay_at(part, False, zz * RING), y, y_minus, y_plus, y_far, to_ym, to_yp
        )

    def along_z(part, yy):
        return RingGather(
            w, lay_at(part, True, yy), z, z_minus, z_plus, z_far, to_zm, to_zp
        )

    first_p, first_q = along_y(0, z), along_z(1, y)
    second_p = [along_z(0, yy) for yy in (y, y_minus, y_plus, y_far)]
    second_q = [along_y(1, zz) for zz in (z, z_minus, z_plus, z_far)]
    first_p.start()
    first_q.start()
    second_p[0].start()
    second_q[0].start()

    unit_base = w.take(8)
    x_base = w.take(12)

    def unit(q, zp, cp):
        for i in range(2):
            block = lay[zp * RING + cp * 2 + i, q * half_rows:(q + 1) * half_rows, :]
            stage[q, cp, zp, i * half_rows:(i + 1) * half_rows, :] = dot(
                block, wqkv[...]
            ).astype(BF)

        @pl.when(cp != c)
        def _():
            w.send(
                unit_base + q * RING + zp, stage.at[q, cp, zp], d2dp.at[q, zp], to_sib,
                keep=False,
            )

    lo, hi = pl.ds(0, half_rows), pl.ds(half_rows, half_rows)

    def settle(q, zp):
        b = x_base + q * 6
        w.arrived(unit_base + q * RING + zp, d2dp.at[q, zp], to_sib)
        stage[q, c, zp] = (
            stage[q, c, zp].astype(F32) + d2dp[q, zp].astype(F32)
        ).astype(BF)
        d = wrap(zp - x)

        @pl.when(d == 2)
        def _():
            w.send(b, stage.at[q, c, zp, hi], hl.at[q], to_right, keep=False)
            w.send(b + 1, stage.at[q, c, zp, lo], hr.at[q], to_left, keep=False)

        @pl.when(d == 1)
        def _():
            w.send(b + 2, stage.at[q, c, zp, lo], fl.at[q, lo], to_right, keep=False)

        @pl.when(d == 3)
        def _():
            w.send(b + 3, stage.at[q, c, zp, hi], fr.at[q, hi], to_left, keep=False)

    def pass_on(q):
        b = x_base + q * 6
        zr, zl = wrap(x + 1), wrap(x - 1)
        w.arrived(b, hl.at[q], to_right)
        stage[q, c, zr, hi] = (
            stage[q, c, zr, hi].astype(F32) + hl[q].astype(F32)
        ).astype(BF)
        w.send(b + 4, stage.at[q, c, zr, hi], fl.at[q, hi], to_right, keep=False)
        w.arrived(b + 1, hr.at[q], to_left)
        stage[q, c, zl, lo] = (
            stage[q, c, zl, lo].astype(F32) + hr[q].astype(F32)
        ).astype(BF)
        w.send(b + 5, stage.at[q, c, zl, lo], fr.at[q, lo], to_left, keep=False)

    def finish(q):
        b = x_base + q * 6
        w.arrived(b + 2, fl.at[q, lo], to_right)
        w.arrived(b + 3, fr.at[q, hi], to_left)
        w.arrived(b + 4, fl.at[q, hi], to_right)
        w.arrived(b + 5, fr.at[q, lo], to_left)
        total = (
            stage[q, c, x].astype(F32) + fl[q].astype(F32) + fr[q].astype(F32)
        ).astype(BF)
        for i in range(2):
            first = i * n_tok + q * half_rows
            projected[first:first + half_rows, :] = total[i * half_rows:(i + 1) * half_rows]

    z_order = (z, z_plus, z_minus, z_far)
    pair = y // 2

    first_p.forward()
    first_q.forward()
    second_p[0].forward()
    second_q[0].forward()
    first_p.near()
    first_q.near()
    for k in (1, 2):
        second_p[k].start()
        second_q[k].start()
    reduce_b.forward()
    second_q[0].near()
    unit(0, z, pair)
    unit(1, z, pair)
    first_p.last()
    first_q.last()
    second_p[3].start()
    second_q[3].start()
    unit(0, z, 1 - pair)
    for k in (1, 2):
        second_p[k].forward()
        second_q[k].forward()
    settle(0, z)

    @pl.when(pair == c)
    def _():
        settle(1, z)

    back_b = send_back(1, reduce_b.result())
    for k in (1, 2):
        second_q[k].near()
    unit(1, z_plus, pair)
    unit(1, z_minus, pair)
    second_p[3].forward()
    second_q[3].forward()
    second_q[3].near()
    unit(1, z_far, pair)
    for k in range(4):
        second_p[k].near()
    for zp in (z_plus, z_minus):
        unit(0, zp, 0)
        unit(0, zp, 1)

    @pl.when(pair == c)
    def _():
        for zp in (z_plus, z_minus, z_far):
            settle(1, zp)

    for zp in (z_plus, z_minus):
        settle(0, zp)
    for k in range(4):
        second_p[k].last()
    unit(0, z_far, 0)
    unit(0, z_far, 1)
    for k in range(4):
        second_q[k].last()
    for zp in z_order:
        unit(1, zp, 1 - pair)
    settle(0, z_far)

    @pl.when(pair == c)
    def _():
        pass_on(1)

    pass_on(0)

    @pl.when(pair != c)
    def _():
        for zp in z_order:
            settle(1, zp)

    load_ups.wait()
    back_rows = scatter(returned(1, back_b))
    grad_tokens[...] = (ups[...].astype(F32) + back_rows).astype(BF)

    @pl.when(pair != c)
    def _():
        pass_on(1)

    finish(0)
    finish(1)

    for copy in w.sent:
        copy.wait_send()
    exchange_end(ex_f, recv_f)
    exchange_end(ex_b, recv_b)
    exchange_end(back_f, ret_r.at[0])
    exchange_end(back_b, ret_r.at[1])

    for q in range(2):
        for k in range(RING):
            w.copy(unit_base + q * RING + k, d2dp.at[q, k], d2dp.at[q, k], to_sib).wait_send()
        for k in range(6):
            w.copy(x_base + q * 6 + k, hl.at[q], hl.at[q], to_left).wait_send()
    save_rows.wait()
    save_hid.wait()
    save_rgrad.wait()
    save_pgr.wait()


def weight_grad_kernel(
    rows, rgrad, hidden, pgrad, products, grads, grad_in, grad_out, projected, grad_tokens
):
    grad_in[0] = dot(rows[0], pgrad[...], TN).astype(BF)
    grad_out[0] = dot(hidden[...], rgrad[0], TN).astype(BF)
    grad_tokens[...] = grads[...]
    blocks = products.shape[1] // 128
    turn = row_permutation(blocks, False)
    for f in range(0, products.shape[0], BAND):
        block = products[f:f + BAND, :]
        stacked = jnp.concatenate(
            [block[:, k * 128:(k + 1) * 128] for k in range(blocks)], axis=0
        )
        projected[f * blocks:(f + BAND) * blocks, :] = dot(turn, stacked).astype(BF)


def on_device(tokens, picked, counts, combine, w_in, w_out, w_qkv, upstream):
    n_tok, width = tokens.shape
    experts, cap = picked.shape[0], picked.shape[2]
    parts, shards = 8, 16
    slice_w = width // parts
    rows = experts * cap
    hidden = w_in.shape[2]
    heads, kinds, lanes = w_qkv.shape[1:]
    columns = heads * kinds * lanes
    flat = w_qkv.transpose(0, 2, 1, 3).reshape(slice_w * kinds * heads, lanes)
    half = n_tok // 2
    anywhere = pl.BlockSpec(memory_space=pl.ANY)
    vmem = pl.BlockSpec(memory_space=pltpu.VMEM)
    smem = pl.BlockSpec(memory_space=pltpu.SMEM)
    sems = 340
    out = pl.pallas_call(
        layer_kernel,
        out_shape=(
            jax.ShapeDtypeStruct((2 * n_tok, columns), BF),
            jax.ShapeDtypeStruct((n_tok, slice_w), BF),
            jax.ShapeDtypeStruct((parts, rows, slice_w), BF),
            jax.ShapeDtypeStruct((parts, rows, slice_w), BF),
            jax.ShapeDtypeStruct((rows, hidden), BF),
            jax.ShapeDtypeStruct((rows, hidden), BF),
        ),
        in_specs=[anywhere] * 5 + [vmem, smem, vmem],
        out_specs=[vmem, vmem] + [anywhere] * 4,
        scratch_shapes=[
            pltpu.VMEM((n_tok, slice_w), BF),
            pltpu.VMEM((n_tok, slice_w), BF),
            pltpu.VMEM((n_tok, width // 2), BF),
            pltpu.VMEM((width, hidden), BF),
            pltpu.VMEM((hidden, width), BF),
            pltpu.VMEM(flat.shape, BF),
            pltpu.VMEM((slice_w, columns), BF),
            pltpu.VMEM((n_tok, rows), BF),
            pltpu.VMEM((rows, shards * cap), BF),
            pltpu.VMEM((rows, 1), F32),
            pltpu.VMEM((experts, cap, slice_w), BF),
            pltpu.VMEM((experts, cap, width // 2), BF),
            pltpu.VMEM((shards, cap, slice_w), BF),
            pltpu.VMEM((shards, cap, width // 2), BF),
            pltpu.VMEM((parts, rows, slice_w), BF),
            pltpu.VMEM((parts, rows, slice_w), BF),
            pltpu.VMEM((rows, hidden), F32),
            pltpu.VMEM((rows, hidden), F32),
            pltpu.VMEM((rows, hidden), BF),
            pltpu.VMEM((rows, hidden), BF),
            pltpu.VMEM((2, RING, rows, slice_w), BF),
            pltpu.VMEM((2, RING, rows, slice_w), BF),
            pltpu.VMEM((2, RING, rows, slice_w), BF),
            pltpu.VMEM((2, rows // 2, slice_w), BF),
            pltpu.VMEM((2, rows // 2, slice_w), BF),
            pltpu.VMEM((2, rows, slice_w), BF),
            pltpu.VMEM((2, rows, slice_w), BF),
            pltpu.VMEM((2, shards, cap, slice_w), BF),
            pltpu.VMEM((2, shards, cap, slice_w), BF),
            pltpu.VMEM((shards, n_tok, slice_w), BF),
            pltpu.VMEM((2, 2, RING, n_tok, columns), BF),
            pltpu.VMEM((2, RING, n_tok, columns), BF),
            pltpu.VMEM((2, half, columns), BF),
            pltpu.VMEM((2, half, columns), BF),
            pltpu.VMEM((2, n_tok, columns), BF),
            pltpu.VMEM((2, n_tok, columns), BF),
            pltpu.SemaphoreType.DMA((10,)),
            pltpu.SemaphoreType.DMA((sems,)),
            pltpu.SemaphoreType.DMA((sems,)),
        ],
        compiler_params=pltpu.CompilerParams(
            collective_id=0, has_side_effects=True, vmem_limit_bytes=62 * 1024 * 1024
        ),
        cost_estimate=pl.CostEstimate(
            flops=8 * 10**9, bytes_accessed=20 * 10**6, transcendentals=3 * 10**5
        ),
        name="moe_layer",
    )(
        tokens, upstream, w_in, w_out, flat,
        picked[:, 0, :], counts, combine[:, 0, :],
    )
    products, grads, taken, row_grad, hid, preact_grad = out
    whole = lambda shape: pl.BlockSpec(shape, lambda j: (0, 0))
    slab = lambda *shape: pl.BlockSpec(shape, lambda j: (j, 0))
    step, grad_step = 2 * n_tok // parts, n_tok // parts
    grad_in, grad_out, projected, grad_tokens = pl.pallas_call(
        weight_grad_kernel,
        grid=(parts,),
        out_shape=(
            jax.ShapeDtypeStruct(w_in.shape, BF),
            jax.ShapeDtypeStruct(w_out.shape, BF),
            jax.ShapeDtypeStruct((2 * n_tok * kinds * heads, lanes), BF),
            jax.ShapeDtypeStruct((n_tok, slice_w), BF),
        ),
        in_specs=[
            pl.BlockSpec((1, rows, slice_w), lambda j: (j, 0, 0)),
            pl.BlockSpec((1, rows, slice_w), lambda j: (j, 0, 0)),
            whole((rows, hidden)),
            whole((rows, hidden)),
            slab(step, columns),
            slab(grad_step, slice_w),
        ],
        out_specs=(
            pl.BlockSpec((1, slice_w, hidden), lambda j: (0, j, 0)),
            pl.BlockSpec((1, hidden, slice_w), lambda j: (0, 0, j)),
            slab(step * kinds * heads, lanes),
            slab(grad_step, slice_w),
        ),
        compiler_params=pltpu.CompilerParams(vmem_limit_bytes=60 * 1024 * 1024),
        cost_estimate=pl.CostEstimate(
            flops=2 * 10**9, bytes_accessed=15 * 10**6, transcendentals=0
        ),
        name="weight_grads",
    )(taken, row_grad, hid, preact_grad, products, grads)
    projected = projected.reshape(2 * n_tok, kinds, heads, lanes).transpose(0, 2, 1, 3)
    return projected, grad_tokens, grad_in, grad_out


def solution(mesh):
    return jax.shard_map(
        on_device,
        mesh=mesh,
        in_specs=(
            P("expert", None),
            P(None, "expert", None),
            P(),
            P(None, "expert", None),
            P("expert", None, "tensor"),
            P("expert", "tensor", None),
            P("tensor", "expert", None, None),
            P("expert", None),
        ),
        out_specs=(
            P("tensor", "expert", None, None),
            P("expert", "tensor"),
            P("expert", None, "tensor"),
            P("expert", "tensor", None),
        ),
        check_vma=False,
    )
```

```python
import jax
import jax.numpy as jnp
from jax import lax
from jax.experimental import pallas as pl
from jax.experimental.pallas import tpu as pltpu
from jax.sharding import PartitionSpec as P

BF = jnp.bfloat16
F32 = jnp.float32
NN = (((1,), (0,)), ((), ()))
NT = (((1,), (1,)), ((), ()))
TN = (((0,), (0,)), ((), ()))
RING = 4
BAND = 32


def dot(a, b, dims=NN):
    return lax.dot_general(a, b, dims, preferred_element_type=F32)


def row_permutation(blocks, gather):
    n = BAND * blocks
    a = lax.broadcasted_iota(jnp.int32, (n, n), 0)
    b = lax.broadcasted_iota(jnp.int32, (n, n), 1)
    if not gather:
        a, b = b, a
    return jnp.where((a % BAND) * blocks + a // BAND == b, 1.0, 0.0).astype(BF)


class Wires:
    def __init__(self, send_sems, recv_sems):
        self.send_sems, self.recv_sems = send_sems, recv_sems
        self.next = 0
        self.sent = []

    def take(self, count=1):
        first = self.next
        self.next += count
        return first

    def copy(self, slot, src, dst, device):
        return pltpu.make_async_remote_copy(
            src_ref=src,
            dst_ref=dst,
            send_sem=self.send_sems.at[slot],
            recv_sem=self.recv_sems.at[slot],
            device_id=device,
            device_id_type=pl.DeviceIdType.MESH,
        )

    def send(self, slot, src, dst, device, keep=True):
        copy = self.copy(slot, src, dst, device)
        copy.start()
        if keep:
            self.sent.append(copy)

    def arrived(self, slot, dst, device):
        self.copy(slot, dst, dst, device).wait_recv()


class RingGather:
    def __init__(self, wires, at, me, minus, plus, far, to_minus, to_plus):
        self.w, self.at = wires, at
        self.me, self.minus, self.plus, self.far = me, minus, plus, far
        self.to_minus, self.to_plus = to_minus, to_plus
        self.base = wires.take(6)

    def start(self):
        b = self.base
        for i, half in enumerate((1, 0)):
            ref = self.at(self.me, half)
            self.w.send(b + i, ref, ref, self.to_plus)
            ref = self.at(self.me, 1 - half)
            self.w.send(b + 3 + i, ref, ref, self.to_minus)

    def forward(self):
        b = self.base
        ref = self.at(self.minus, 1)
        self.w.arrived(b, ref, self.to_plus)
        self.w.send(b + 2, ref, ref, self.to_plus)
        ref = self.at(self.plus, 0)
        self.w.arrived(b + 3, ref, self.to_minus)
        self.w.send(b + 5, ref, ref, self.to_minus)

    def near(self):
        self.w.arrived(self.base + 1, self.at(self.minus, 0), self.to_plus)
        self.w.arrived(self.base + 4, self.at(self.plus, 1), self.to_minus)

    def last(self):
        self.w.arrived(self.base + 2, self.at(self.far, 1), self.to_plus)
        self.w.arrived(self.base + 5, self.at(self.far, 0), self.to_minus)


def layer_kernel(
    tokens, upstream, w_in, w_out, w_qkv, picked, counts, combine,
    projected, grad_tokens, grad_in, grad_out,
    tok, ups, ups_half, win, wout, wraw, wqkv, sel, comp, wcol,
    send_f, send_b, recv_f, recv_b, ag_f, ag_b,
    acc, slope, hid, pgr,
    pst, d2d, sbuf, half_l, half_r, full_l, full_r,
    ret_s, ret_r, lay, stage, d2dp, hl, hr, fl, fr,
    load_sems, send_sems, recv_sems,
):
    s, t = lax.axis_index("expert"), lax.axis_index("tensor")
    z, y = s // RING, s % RING
    x, c = t // 2, t % 2
    shards, experts, cap = 16, counts.shape[0], combine.shape[1]
    n_tok, width = tok.shape
    half_rows = n_tok // 2
    quarter = n_tok // 4

    def wrap(v):
        return lax.rem(v + RING, RING)

    left, right = wrap(x - 1) * 2 + c, wrap(x + 1) * 2 + c
    far = wrap(x + 2) * 2 + c
    sib = x * 2 + 1 - c
    to_left, to_right, to_sib = (s, left), (s, right), (s, sib)
    y_minus, y_plus, y_far = wrap(y - 1), wrap(y + 1), wrap(y + 2)
    z_minus, z_plus, z_far = wrap(z - 1), wrap(z + 1), wrap(z + 2)
    to_ym, to_yp = (z * RING + y_minus, t), (z * RING + y_plus, t)
    to_zm, to_zp = (z_minus * RING + y, t), (z_plus * RING + y, t)

    cols = pl.ds(pl.multiple_of(t * width, width), width)
    load_tok = pltpu.make_async_copy(tokens.at[:, cols], tok, load_sems.at[0])
    load_ups = pltpu.make_async_copy(upstream.at[:, cols], ups, load_sems.at[1])
    load_win = pltpu.make_async_copy(w_in.at[0], win, load_sems.at[2])
    load_wout = pltpu.make_async_copy(w_out.at[0], wout, load_sems.at[3])
    wide_cols = pl.ds(pl.multiple_of(c * RING * width, width), RING * width)
    load_half = pltpu.make_async_copy(upstream.at[:, wide_cols], ups_half, load_sems.at[4])
    load_qkv = pltpu.make_async_copy(w_qkv, wraw, load_sems.at[5])
    load_tok.start()
    load_half.start()
    load_win.start()
    load_wout.start()
    load_qkv.start()
    load_ups.start()

    barrier = pltpu.get_barrier_semaphore()

    def greet(i, carry):
        pl.semaphore_signal(
            barrier, inc=1, device_id=(lax.rem(s + i, shards), t),
            device_id_type=pl.DeviceIdType.MESH,
        )
        return carry

    lax.fori_loop(1, shards, greet, 0)
    for device in (to_left, to_right, to_sib):
        pl.semaphore_signal(
            barrier, inc=1, device_id=device, device_id_type=pl.DeviceIdType.MESH
        )

    slots = experts * cap
    lane = lax.broadcasted_iota(jnp.int32, (1, slots), 1)
    spread = (
        lax.broadcasted_iota(jnp.int32, (cap, slots), 1) % cap
        == lax.broadcasted_iota(jnp.int32, (cap, slots), 0)
    )
    spread = jnp.where(spread, 1.0, 0.0).astype(BF)
    wide = dot(picked[...].astype(F32).astype(BF), spread)
    own_row = (
        lax.broadcasted_iota(jnp.int32, (experts, slots), 1) // cap
        == lax.broadcasted_iota(jnp.int32, (experts, slots), 0)
    )
    pick_row = jnp.sum(jnp.where(own_row, wide, 0.0), axis=0, keepdims=True).astype(jnp.int32)
    count_row = jnp.zeros((1, slots), jnp.int32)
    for e in range(experts):
        count_row = jnp.where(lane // cap == e, counts[e, s], count_row)
    pick_row = jnp.where(lane % cap < count_row, pick_row, -1)
    token_ids = lax.broadcasted_iota(jnp.int32, (n_tok, slots), 0)
    sel[...] = jnp.where(token_ids == pick_row, 1.0, 0.0).astype(BF)

    load_tok.wait()
    send_f[...] = dot(sel[...], tok[...], TN).astype(BF).reshape(send_f.shape)

    pl.semaphore_wait(barrier, shards - 1 + 3)

    w = Wires(send_sems, recv_sems)

    def exchange(src_at, recv):
        base = w.take(shards)

        def body(i, carry):
            to = lax.rem(s + i, shards)
            w.send(base + i, src_at(to), recv.at[s], (to, t), keep=False)
            return carry

        lax.fori_loop(1, shards, body, 0)
        recv[s] = src_at(s)[...]
        return base

    def exchanged(base, recv):
        def body(i, carry):
            source = lax.rem(s - i + shards, shards)
            w.arrived(base + i, recv.at[source], (source, t))
            return carry

        lax.fori_loop(1, shards, body, 0)

    def exchange_end(base, recv):
        def body(i, carry):
            w.copy(base + i, recv.at[0], recv.at[0], to_sib).wait_send()
            return carry

        lax.fori_loop(1, shards, body, 0)

    ex_f = exchange(lambda to: send_f.at[to // 2], recv_f)

    eye = (
        lax.broadcasted_iota(jnp.int32, (cap, cap), 0)
        == lax.broadcasted_iota(jnp.int32, (cap, cap), 1)
    )
    turned = lax.dot_general(
        jnp.where(eye, 1.0, 0.0).astype(F32), combine[...], NT,
        precision=lax.Precision.HIGHEST, preferred_element_type=F32,
    )
    for e in range(experts):
        wcol[e * cap:(e + 1) * cap, :] = turned[:, e:e + 1]

    padded = shards * cap
    lane = lax.broadcasted_iota(jnp.int32, (1, padded), 1)
    mine = s // 2
    offset = jnp.int32(0)
    offset_row = jnp.zeros((1, padded), jnp.int32)
    count_row = jnp.zeros((1, padded), jnp.int32)
    for shard in range(shards):
        count = counts[mine, shard]
        here = lane // cap == shard
        offset_row = jnp.where(here, offset, offset_row)
        count_row = jnp.where(here, count, count_row)
        offset = offset + count
    position = jnp.where(lane % cap < count_row, offset_row + lane % cap, -1)
    row_ids = lax.broadcasted_iota(jnp.int32, comp.shape, 0)
    comp[...] = jnp.where(row_ids == position, 1.0, 0.0).astype(BF)

    load_half.wait()
    for k in range(RING):
        part = slice(k * width, (k + 1) * width)
        taken = dot(sel[...], ups_half[:, part], TN) * wcol[...]
        send_b[:, :, part] = taken.astype(BF).reshape(experts, cap, width)

    load_qkv.wait()
    blocks = wqkv.shape[1] // 128
    turn = row_permutation(blocks, True)
    for f in range(0, width, BAND):
        moved = dot(turn, wraw[f * blocks:(f + BAND) * blocks, :]).astype(BF)
        for k in range(blocks):
            wqkv[f:f + BAND, k * 128:(k + 1) * 128] = moved[k * BAND:(k + 1) * BAND]

    class RowGather:
        def __init__(self, buf):
            self.buf = buf

            def at(block, half):
                return buf.at[block, pl.ds(half * half_rows, half_rows), :]

            self.ring = RingGather(w, at, t, left, right, far, to_left, to_right)
            self.base = w.take(7)
            self.at = at

        def give(self, k, ref):
            w.send(self.base + k, ref, ref, to_sib)

        def start(self):
            self.ring.start()
            self.give(0, self.buf.at[t])

        def forward(self):
            self.ring.forward()
            self.give(1, self.at(left, 1))
            self.give(2, self.at(right, 0))

        def near(self):
            self.ring.near()
            self.give(3, self.at(left, 0))
            self.give(4, self.at(right, 1))

        def last(self):
            self.ring.last()
            self.give(5, self.at(far, 1))
            self.give(6, self.at(far, 0))

        def sib_own(self):
            w.arrived(self.base, self.buf.at[sib], to_sib)

        def sib_near(self):
            other = 1 - 2 * c
            for k, (block, half) in enumerate(((left, 1), (right, 0), (left, 0), (right, 1))):
                w.arrived(self.base + 1 + k, self.at(block + other, half), to_sib)

        def sib_last(self):
            other = 1 - 2 * c
            w.arrived(self.base + 5, self.at(far + other, 1), to_sib)
            w.arrived(self.base + 6, self.at(far + other, 0), to_sib)

    other = 1 - 2 * c

    def win_at(j):
        return win[pl.ds(pl.multiple_of(j * width, width), width), :]

    def wout_at(j):
        return wout[:, pl.ds(pl.multiple_of(j * width, width), width)]

    def gathered(gather, weight_at, dims):
        buf = gather.buf

        def add(j, first=False):
            term = dot(buf[j], weight_at(j), dims)
            if first:
                acc[...] = term
            else:
                acc[...] += term

        add(t, True)
        gather.sib_own()
        add(sib)
        gather.near()
        add(left)
        add(right)
        gather.last()
        gather.sib_near()
        add(left + other)
        add(right + other)
        add(far)
        gather.sib_last()
        add(far + other)

    class RowReduce:
        def __init__(self, k):
            self.k = k
            self.base = w.take(10)

        def partials(self, lhs, weight_at, dims):
            k, b = self.k, self.base
            for d in (2, 1, 3, 0):
                j = wrap(x + d) * 2 + 1 - c
                pst[k, d] = dot(lhs[...], weight_at(j), dims).astype(BF)
                w.send(b + d, pst.at[k, d], d2d.at[k, d], to_sib)
            lo, hi = pl.ds(0, half_rows), pl.ds(half_rows, half_rows)
            for d in (2, 1, 3, 0):
                j = wrap(x + d) * 2 + c
                own = dot(lhs[...], weight_at(j), dims)
                w.arrived(b + d, d2d.at[k, d], to_sib)
                sbuf[k, d] = (own + d2d[k, d].astype(F32)).astype(BF)
                if d == 2:
                    w.send(b + 4, sbuf.at[k, d, hi], half_l.at[k], to_right)
                    w.send(b + 5, sbuf.at[k, d, lo], half_r.at[k], to_left)
                elif d == 1:
                    w.send(b + 6, sbuf.at[k, d, lo], full_l.at[k, lo], to_right)
                elif d == 3:
                    w.send(b + 7, sbuf.at[k, d, hi], full_r.at[k, hi], to_left)

        def forward(self):
            k, b = self.k, self.base
            lo, hi = pl.ds(0, half_rows), pl.ds(half_rows, half_rows)
            w.arrived(b + 4, half_l.at[k], to_right)
            sbuf[k, 1, hi] = (sbuf[k, 1, hi].astype(F32) + half_l[k].astype(F32)).astype(BF)
            w.send(b + 8, sbuf.at[k, 1, hi], full_l.at[k, hi], to_right)
            w.arrived(b + 5, half_r.at[k], to_left)
            sbuf[k, 3, lo] = (sbuf[k, 3, lo].astype(F32) + half_r[k].astype(F32)).astype(BF)
            w.send(b + 9, sbuf.at[k, 3, lo], full_r.at[k, lo], to_left)

        def result(self):
            k, b = self.k, self.base
            lo, hi = pl.ds(0, half_rows), pl.ds(half_rows, half_rows)
            w.arrived(b + 6, full_l.at[k, lo], to_right)
            w.arrived(b + 7, full_r.at[k, hi], to_left)
            w.arrived(b + 8, full_l.at[k, hi], to_right)
            w.arrived(b + 9, full_r.at[k, lo], to_left)
            total = sbuf[k, 0].astype(F32) + full_l[k].astype(F32) + full_r[k].astype(F32)
            return total.astype(BF)

    def send_back(k, rows):
        ret_s[k] = dot(comp[...], rows, TN).astype(BF).reshape(ret_s.shape[1:])
        return exchange(lambda to: ret_s.at[k, to], ret_r.at[k])

    def returned(k, base):
        exchanged(base, ret_r.at[k])
        pairs = ret_r[k].reshape(experts, 2, cap, width).astype(F32)
        return (pairs[:, 0] + pairs[:, 1]).reshape(slots, width)

    def scatter(values):
        high = values.astype(BF)
        low = (values - high.astype(F32)).astype(BF)
        return dot(sel[...], high) + dot(sel[...], low)

    gather_f = RowGather(ag_f)
    exchanged(ex_f, recv_f)
    ag_f[t] = dot(comp[...], recv_f[...].reshape(padded, width)).astype(BF)
    gather_f.start()
    ex_b = exchange(lambda to: send_b.at[to // 2], recv_b)
    gather_f.forward()
    load_win.wait()
    gathered(gather_f, win_at, NN)
    pre = acc[...]
    cdf = 0.5 * (1.0 + lax.erf(pre * 0.7071067811865476))
    hid[...] = (pre * cdf).astype(BF)
    slope[...] = cdf + pre * jnp.exp(-0.5 * pre * pre) * 0.3989422804014327
    load_wout.wait()
    reduce_f = RowReduce(0)
    reduce_f.partials(hid, wout_at, NN)


    reduce_f.forward()
    back_f = send_back(0, reduce_f.result())

    give_b = w.take(RING)
    exchanged(ex_b, recv_b)
    for k in range(RING):
        part = recv_b[:, :, k * width:(k + 1) * width].reshape(padded, width)
        mine_k = ag_b.at[c * RING + k]
        mine_k[...] = dot(comp[...], part).astype(BF)
        w.send(give_b + k, mine_k, mine_k, to_sib)
    for k in range(2 * RING):
        j = c * RING + k if k < RING else (1 - c) * RING + k - RING
        if k >= RING:
            w.arrived(give_b + k - RING, ag_b.at[j], to_sib)
        term = dot(ag_b[j], wout_at(j), NT)
        if k == 0:
            acc[...] = term
        else:
            acc[...] += term
    pgr[...] = (acc[...] * slope[...]).astype(BF)
    halves = returned(0, back_f)
    mixture = scatter(halves * wcol[...])
    lay[s] = (tok[...].astype(F32) + mixture).astype(BF)

    def lay_at(part, along_z, fixed):
        def at(pos, half):
            index = pos * RING + fixed if along_z else fixed + pos
            return lay.at[index, pl.ds(part * half_rows + half * quarter, quarter), :]
        return at

    def along_y(part, zz):
        return RingGather(
            w, lay_at(part, False, zz * RING), y, y_minus, y_plus, y_far, to_ym, to_yp
        )

    def along_z(part, yy):
        return RingGather(
            w, lay_at(part, True, yy), z, z_minus, z_plus, z_far, to_zm, to_zp
        )

    first_p, first_q = along_y(0, z), along_z(1, y)
    second_p = [along_z(0, yy) for yy in (y, y_minus, y_plus, y_far)]
    second_q = [along_y(1, zz) for zz in (z, z_minus, z_plus, z_far)]
    first_p.start()
    first_q.start()
    second_p[0].start()
    second_q[0].start()

    reduce_b = RowReduce(1)
    reduce_b.partials(pgr, win_at, NT)

    unit_base = w.take(8)
    x_base = w.take(12)

    def unit(q, zp, cp):
        for i in range(2):
            block = lay[zp * RING + cp * 2 + i, q * half_rows:(q + 1) * half_rows, :]
            stage[q, cp, zp, i * half_rows:(i + 1) * half_rows, :] = dot(
                block, wqkv[...]
            ).astype(BF)

        @pl.when(cp != c)
        def _():
            w.send(
                unit_base + q * RING + zp, stage.at[q, cp, zp], d2dp.at[q, zp], to_sib,
                keep=False,
            )

    lo, hi = pl.ds(0, half_rows), pl.ds(half_rows, half_rows)

    def settle(q, zp):
        b = x_base + q * 6
        w.arrived(unit_base + q * RING + zp, d2dp.at[q, zp], to_sib)
        stage[q, c, zp] = (
            stage[q, c, zp].astype(F32) + d2dp[q, zp].astype(F32)
        ).astype(BF)
        d = wrap(zp - x)

        @pl.when(d == 2)
        def _():
            w.send(b, stage.at[q, c, zp, hi], hl.at[q], to_right, keep=False)
            w.send(b + 1, stage.at[q, c, zp, lo], hr.at[q], to_left, keep=False)

        @pl.when(d == 1)
        def _():
            w.send(b + 2, stage.at[q, c, zp, lo], fl.at[q, lo], to_right, keep=False)

        @pl.when(d == 3)
        def _():
            w.send(b + 3, stage.at[q, c, zp, hi], fr.at[q, hi], to_left, keep=False)

    def pass_on(q):
        b = x_base + q * 6
        zr, zl = wrap(x + 1), wrap(x - 1)
        w.arrived(b, hl.at[q], to_right)
        stage[q, c, zr, hi] = (
            stage[q, c, zr, hi].astype(F32) + hl[q].astype(F32)
        ).astype(BF)
        w.send(b + 4, stage.at[q, c, zr, hi], fl.at[q, hi], to_right, keep=False)
        w.arrived(b + 1, hr.at[q], to_left)
        stage[q, c, zl, lo] = (
            stage[q, c, zl, lo].astype(F32) + hr[q].astype(F32)
        ).astype(BF)
        w.send(b + 5, stage.at[q, c, zl, lo], fr.at[q, lo], to_left, keep=False)

    def finish(q):
        b = x_base + q * 6
        w.arrived(b + 2, fl.at[q, lo], to_right)
        w.arrived(b + 3, fr.at[q, hi], to_left)
        w.arrived(b + 4, fl.at[q, hi], to_right)
        w.arrived(b + 5, fr.at[q, lo], to_left)
        total = (
            stage[q, c, x].astype(F32) + fl[q].astype(F32) + fr[q].astype(F32)
        ).astype(BF)
        for i in range(2):
            first = i * n_tok + q * half_rows
            projected[first:first + half_rows, :] = total[i * half_rows:(i + 1) * half_rows]

    z_order = (z, z_plus, z_minus, z_far)
    pair = y // 2

    first_p.forward()
    first_q.forward()
    second_p[0].forward()
    second_q[0].forward()
    first_p.near()
    first_q.near()
    for k in (1, 2):
        second_p[k].start()
        second_q[k].start()
    second_q[0].near()
    unit(0, z, pair)
    unit(1, z, pair)
    first_p.last()
    first_q.last()
    second_p[3].start()
    second_q[3].start()
    unit(0, z, 1 - pair)
    for k in (1, 2):
        second_p[k].forward()
        second_q[k].forward()
    reduce_b.forward()
    settle(0, z)

    @pl.when(pair == c)
    def _():
        settle(1, z)

    for j in range(2 * RING):
        part = slice(j * width, (j + 1) * width)
        grad_in[part, :] = dot(ag_f[j], pgr[...], TN).astype(BF)
    for k in (1, 2):
        second_q[k].near()
    unit(1, z_plus, pair)
    unit(1, z_minus, pair)
    second_p[3].forward()
    second_q[3].forward()
    back_b = send_back(1, reduce_b.result())
    second_q[3].near()
    unit(1, z_far, pair)
    hid_turned = hid[...].T
    for j in range(2 * RING):
        part = slice(j * width, (j + 1) * width)
        grad_out[:, part] = dot(hid_turned, ag_b[j]).astype(BF)
    for k in range(4):
        second_p[k].near()
    for zp in (z_plus, z_minus):
        unit(0, zp, 0)
        unit(0, zp, 1)

    @pl.when(pair == c)
    def _():
        for zp in (z_plus, z_minus, z_far):
            settle(1, zp)

    for zp in (z_plus, z_minus):
        settle(0, zp)
    for k in range(4):
        second_p[k].last()
    unit(0, z_far, 0)
    unit(0, z_far, 1)
    for k in range(4):
        second_q[k].last()
    for zp in z_order:
        unit(1, zp, 1 - pair)
    settle(0, z_far)

    @pl.when(pair == c)
    def _():
        pass_on(1)

    pass_on(0)

    @pl.when(pair != c)
    def _():
        for zp in z_order:
            settle(1, zp)

    load_ups.wait()
    back_rows = scatter(returned(1, back_b))
    grad_tokens[...] = (ups[...].astype(F32) + back_rows).astype(BF)

    @pl.when(pair != c)
    def _():
        pass_on(1)

    finish(0)
    finish(1)

    for copy in w.sent:
        copy.wait_send()
    exchange_end(ex_f, recv_f)
    exchange_end(ex_b, recv_b)
    exchange_end(back_f, ret_r.at[0])
    exchange_end(back_b, ret_r.at[1])

    for q in range(2):
        for k in range(RING):
            w.copy(unit_base + q * RING + k, d2dp.at[q, k], d2dp.at[q, k], to_sib).wait_send()
        for k in range(6):
            w.copy(x_base + q * 6 + k, hl.at[q], hl.at[q], to_left).wait_send()


def write_kernel(
    grad_in_v, grad_out_v, products, grads, projected, grad_tokens, grad_in, grad_out, sems
):
    copies = []
    for src, dst in ((grad_in_v, grad_in.at[0]), (grad_out_v, grad_out.at[0]), (grads, grad_tokens)):
        copies.append(pltpu.make_async_copy(src, dst, sems.at[len(copies)]))
        copies[-1].start()
    blocks = products.shape[1] // 128
    turn = row_permutation(blocks, False)
    for f in range(0, products.shape[0], BAND):
        block = products[f:f + BAND, :]
        stacked = jnp.concatenate(
            [block[:, k * 128:(k + 1) * 128] for k in range(blocks)], axis=0
        )
        projected[f * blocks:(f + BAND) * blocks, :] = dot(turn, stacked).astype(BF)
    for copy in copies:
        copy.wait()


def on_device(tokens, picked, counts, combine, w_in, w_out, w_qkv, upstream):
    n_tok, width = tokens.shape
    experts, cap = picked.shape[0], picked.shape[2]
    parts, shards = 8, 16
    slice_w = width // parts
    rows = experts * cap
    hidden = w_in.shape[2]
    heads, kinds, lanes = w_qkv.shape[1:]
    columns = heads * kinds * lanes
    flat = w_qkv.transpose(0, 2, 1, 3).reshape(slice_w * kinds * heads, lanes)
    half = n_tok // 2
    anywhere = pl.BlockSpec(memory_space=pl.ANY)
    vmem = pl.BlockSpec(memory_space=pltpu.VMEM)
    smem = pl.BlockSpec(memory_space=pltpu.SMEM)
    sems = 340
    out = pl.pallas_call(
        layer_kernel,
        out_shape=(
            pltpu.VMEM((2 * n_tok, columns), BF),
            pltpu.VMEM((n_tok, slice_w), BF),
            pltpu.VMEM((width, hidden), BF),
            pltpu.VMEM((hidden, width), BF),
        ),
        in_specs=[anywhere] * 5 + [vmem, smem, vmem],
        out_specs=[vmem] * 4,
        scratch_shapes=[
            pltpu.VMEM((n_tok, slice_w), BF),
            pltpu.VMEM((n_tok, slice_w), BF),
            pltpu.VMEM((n_tok, width // 2), BF),
            pltpu.VMEM((width, hidden), BF),
            pltpu.VMEM((hidden, width), BF),
            pltpu.VMEM(flat.shape, BF),
            pltpu.VMEM((slice_w, columns), BF),
            pltpu.VMEM((n_tok, rows), BF),
            pltpu.VMEM((rows, shards * cap), BF),
            pltpu.VMEM((rows, 1), F32),
            pltpu.VMEM((experts, cap, slice_w), BF),
            pltpu.VMEM((experts, cap, width // 2), BF),
            pltpu.VMEM((shards, cap, slice_w), BF),
            pltpu.VMEM((shards, cap, width // 2), BF),
            pltpu.VMEM((parts, rows, slice_w), BF),
            pltpu.VMEM((parts, rows, slice_w), BF),
            pltpu.VMEM((rows, hidden), F32),
            pltpu.VMEM((rows, hidden), F32),
            pltpu.VMEM((rows, hidden), BF),
            pltpu.VMEM((rows, hidden), BF),
            pltpu.VMEM((2, RING, rows, slice_w), BF),
            pltpu.VMEM((2, RING, rows, slice_w), BF),
            pltpu.VMEM((2, RING, rows, slice_w), BF),
            pltpu.VMEM((2, rows // 2, slice_w), BF),
            pltpu.VMEM((2, rows // 2, slice_w), BF),
            pltpu.VMEM((2, rows, slice_w), BF),
            pltpu.VMEM((2, rows, slice_w), BF),
            pltpu.VMEM((2, shards, cap, slice_w), BF),
            pltpu.VMEM((2, shards, cap, slice_w), BF),
            pltpu.VMEM((shards, n_tok, slice_w), BF),
            pltpu.VMEM((2, 2, RING, n_tok, columns), BF),
            pltpu.VMEM((2, RING, n_tok, columns), BF),
            pltpu.VMEM((2, half, columns), BF),
            pltpu.VMEM((2, half, columns), BF),
            pltpu.VMEM((2, n_tok, columns), BF),
            pltpu.VMEM((2, n_tok, columns), BF),
            pltpu.SemaphoreType.DMA((6,)),
            pltpu.SemaphoreType.DMA((sems,)),
            pltpu.SemaphoreType.DMA((sems,)),
        ],
        compiler_params=pltpu.CompilerParams(
            collective_id=0, has_side_effects=True, vmem_limit_bytes=50 * 1024 * 1024
        ),
        cost_estimate=pl.CostEstimate(
            flops=8 * 10**9, bytes_accessed=20 * 10**6, transcendentals=3 * 10**5
        ),
        name="moe_layer",
    )(
        tokens, upstream, w_in, w_out, flat,
        picked[:, 0, :], counts, combine[:, 0, :],
    )
    products, grads, grad_in, grad_out = out
    projected, grad_tokens, grad_in, grad_out = pl.pallas_call(
        write_kernel,
        out_shape=(
            jax.ShapeDtypeStruct((2 * n_tok * kinds * heads, lanes), BF),
            jax.ShapeDtypeStruct((n_tok, slice_w), BF),
            jax.ShapeDtypeStruct(w_in.shape, BF),
            jax.ShapeDtypeStruct(w_out.shape, BF),
        ),
        in_specs=[vmem] * 4,
        out_specs=(vmem, anywhere, anywhere, anywhere),
        scratch_shapes=[pltpu.SemaphoreType.DMA((3,))],
        compiler_params=pltpu.CompilerParams(vmem_limit_bytes=16 * 1024 * 1024),
        cost_estimate=pl.CostEstimate(
            flops=2 * 10**8, bytes_accessed=18 * 10**6, transcendentals=0
        ),
        name="write_out",
    )(grad_in, grad_out, products, grads)
    projected = projected.reshape(2 * n_tok, kinds, heads, lanes).transpose(0, 2, 1, 3)
    return projected, grad_tokens, grad_in, grad_out


def solution(mesh):
    return jax.shard_map(
        on_device,
        mesh=mesh,
        in_specs=(
            P("expert", None),
            P(None, "expert", None),
            P(),
            P(None, "expert", None),
            P("expert", None, "tensor"),
            P("expert", "tensor", None),
            P("tensor", "expert", None, None),
            P("expert", None),
        ),
        out_specs=(
            P("tensor", "expert", None, None),
            P("expert", "tensor"),
            P("expert", None, "tensor"),
            P("expert", "tensor", None),
        ),
        check_vma=False,
    )
```

```python
import jax
import jax.numpy as jnp
from jax import lax
from jax.experimental import pallas as pl
from jax.experimental.pallas import tpu as pltpu
from jax.sharding import PartitionSpec as P

BF = jnp.bfloat16
F32 = jnp.float32
NN = (((1,), (0,)), ((), ()))
NT = (((1,), (1,)), ((), ()))
TN = (((0,), (0,)), ((), ()))
RING = 4
BAND = 32


def dot(a, b, dims=NN):
    return lax.dot_general(a, b, dims, preferred_element_type=F32)


def row_permutation(blocks, gather):
    n = BAND * blocks
    a = lax.broadcasted_iota(jnp.int32, (n, n), 0)
    b = lax.broadcasted_iota(jnp.int32, (n, n), 1)
    if not gather:
        a, b = b, a
    return jnp.where((a % BAND) * blocks + a // BAND == b, 1.0, 0.0).astype(BF)


class Wires:
    def __init__(self, send_sems, recv_sems):
        self.send_sems, self.recv_sems = send_sems, recv_sems
        self.next = 0
        self.sent = []

    def take(self, count=1):
        first = self.next
        self.next += count
        return first

    def copy(self, slot, src, dst, device):
        return pltpu.make_async_remote_copy(
            src_ref=src,
            dst_ref=dst,
            send_sem=self.send_sems.at[slot],
            recv_sem=self.recv_sems.at[slot],
            device_id=device,
            device_id_type=pl.DeviceIdType.MESH,
        )

    def send(self, slot, src, dst, device, keep=True):
        copy = self.copy(slot, src, dst, device)
        copy.start()
        if keep:
            self.sent.append(copy)

    def arrived(self, slot, dst, device):
        self.copy(slot, dst, dst, device).wait_recv()


class RingGather:
    def __init__(self, wires, at, me, minus, plus, far, to_minus, to_plus):
        self.w, self.at = wires, at
        self.me, self.minus, self.plus, self.far = me, minus, plus, far
        self.to_minus, self.to_plus = to_minus, to_plus
        self.base = wires.take(6)

    def start(self):
        b = self.base
        for i, half in enumerate((1, 0)):
            ref = self.at(self.me, half)
            self.w.send(b + i, ref, ref, self.to_plus)
            ref = self.at(self.me, 1 - half)
            self.w.send(b + 3 + i, ref, ref, self.to_minus)

    def forward(self):
        b = self.base
        ref = self.at(self.minus, 1)
        self.w.arrived(b, ref, self.to_plus)
        self.w.send(b + 2, ref, ref, self.to_plus)
        ref = self.at(self.plus, 0)
        self.w.arrived(b + 3, ref, self.to_minus)
        self.w.send(b + 5, ref, ref, self.to_minus)

    def near(self):
        self.w.arrived(self.base + 1, self.at(self.minus, 0), self.to_plus)
        self.w.arrived(self.base + 4, self.at(self.plus, 1), self.to_minus)

    def last(self):
        self.w.arrived(self.base + 2, self.at(self.far, 1), self.to_plus)
        self.w.arrived(self.base + 5, self.at(self.far, 0), self.to_minus)


def layer_kernel(
    tokens, upstream, w_in, w_out, w_qkv, picked, counts, combine,
    projected, grad_tokens, grad_in, grad_out,
    tok, ups, ups_half, win, wout, wraw, wq, sel, comp, wcol,
    send_f, send_b, recv_f, recv_b, ag_f, ag_b,
    acc, slope, hid, pgr,
    pst, d2d, sbuf, half_l, half_r, full_l, full_r,
    ret_s, ret_r, lay_s, lay, sum_p, sum_q, out_s,
    load_sems, send_sems, recv_sems,
):
    s, t = lax.axis_index("expert"), lax.axis_index("tensor")
    z, y = s // RING, s % RING
    x, c = t // 2, t % 2
    shards, parts = RING * RING, 2 * RING
    experts, cap = counts.shape[0], combine.shape[1]
    n_tok, width = tok.shape
    half_rows = n_tok // 2
    piece = n_tok // parts

    def wrap(v):
        return lax.rem(v + RING, RING)

    left, right = wrap(x - 1) * 2 + c, wrap(x + 1) * 2 + c
    far = wrap(x + 2) * 2 + c
    sib = x * 2 + 1 - c
    to_left, to_right, to_sib = (s, left), (s, right), (s, sib)
    y_minus, y_plus, y_far = wrap(y - 1), wrap(y + 1), wrap(y + 2)
    z_minus, z_plus, z_far = wrap(z - 1), wrap(z + 1), wrap(z + 2)
    to_ym, to_yp = (z * RING + y_minus, t), (z * RING + y_plus, t)
    to_zm, to_zp = (z_minus * RING + y, t), (z_plus * RING + y, t)

    cols = pl.ds(pl.multiple_of(t * width, width), width)
    load_tok = pltpu.make_async_copy(tokens.at[:, cols], tok, load_sems.at[0])
    load_ups = pltpu.make_async_copy(upstream.at[:, cols], ups, load_sems.at[1])
    load_win = pltpu.make_async_copy(w_in.at[0], win, load_sems.at[2])
    load_wout = pltpu.make_async_copy(w_out.at[0], wout, load_sems.at[3])
    wide_cols = pl.ds(pl.multiple_of(c * RING * width, width), RING * width)
    load_half = pltpu.make_async_copy(upstream.at[:, wide_cols], ups_half, load_sems.at[4])
    load_qkv = pltpu.make_async_copy(w_qkv, wraw, load_sems.at[5])
    load_tok.start()
    load_half.start()
    load_win.start()
    load_wout.start()
    load_qkv.start()
    load_ups.start()

    barrier = pltpu.get_barrier_semaphore()

    def greet(i, carry):
        pl.semaphore_signal(
            barrier, inc=1, device_id=(lax.rem(s + i, shards), t),
            device_id_type=pl.DeviceIdType.MESH,
        )
        return carry

    lax.fori_loop(1, shards, greet, 0)

    def greet_line(i, carry):
        pl.semaphore_signal(
            barrier, inc=1, device_id=(s, lax.rem(t + i, parts)),
            device_id_type=pl.DeviceIdType.MESH,
        )
        return carry

    lax.fori_loop(1, parts, greet_line, 0)

    slots = experts * cap
    lane = lax.broadcasted_iota(jnp.int32, (1, slots), 1)
    spread = (
        lax.broadcasted_iota(jnp.int32, (cap, slots), 1) % cap
        == lax.broadcasted_iota(jnp.int32, (cap, slots), 0)
    )
    spread = jnp.where(spread, 1.0, 0.0).astype(BF)
    wide = dot(picked[...].astype(F32).astype(BF), spread)
    own_row = (
        lax.broadcasted_iota(jnp.int32, (experts, slots), 1) // cap
        == lax.broadcasted_iota(jnp.int32, (experts, slots), 0)
    )
    pick_row = jnp.sum(jnp.where(own_row, wide, 0.0), axis=0, keepdims=True).astype(jnp.int32)
    count_row = jnp.zeros((1, slots), jnp.int32)
    for e in range(experts):
        count_row = jnp.where(lane // cap == e, counts[e, s], count_row)
    pick_row = jnp.where(lane % cap < count_row, pick_row, -1)
    token_ids = lax.broadcasted_iota(jnp.int32, (n_tok, slots), 0)
    sel[...] = jnp.where(token_ids == pick_row, 1.0, 0.0).astype(BF)

    load_tok.wait()
    send_f[...] = dot(sel[...], tok[...], TN).astype(BF).reshape(send_f.shape)

    load_qkv.wait()
    blocks = wq.shape[2] // 128
    turn = row_permutation(blocks, True)
    for f in range(0, width, BAND):
        moved = dot(turn, wraw[f * blocks:(f + BAND) * blocks, :]).astype(BF)
        for k in range(blocks):
            wq[t, f:f + BAND, k * 128:(k + 1) * 128] = moved[k * BAND:(k + 1) * BAND]

    pl.semaphore_wait(barrier, shards - 1 + parts - 1)

    w = Wires(send_sems, recv_sems)

    def exchange(src_at, recv):
        base = w.take(shards)

        def body(i, carry):
            to = lax.rem(s + i, shards)
            w.send(base + i, src_at(to), recv.at[s], (to, t), keep=False)
            return carry

        lax.fori_loop(1, shards, body, 0)
        recv[s] = src_at(s)[...]
        return base

    def exchanged(base, recv):
        def body(i, carry):
            source = lax.rem(s - i + shards, shards)
            w.arrived(base + i, recv.at[source], (source, t))
            return carry

        lax.fori_loop(1, shards, body, 0)

    def exchange_end(base, recv):
        def body(i, carry):
            w.copy(base + i, recv.at[0], recv.at[0], to_sib).wait_send()
            return carry

        lax.fori_loop(1, shards, body, 0)

    class RowGather:
        def __init__(self, buf, first, count):
            self.buf = buf
            self.whole = lambda block: buf.at[block, pl.ds(first, count), :]

            def at(block, half):
                return buf.at[block, pl.ds(first + half * count // 2, count // 2), :]

            self.ring = RingGather(w, at, t, left, right, far, to_left, to_right)
            self.base = w.take(7)
            self.at = at

        def give(self, k, ref):
            w.send(self.base + k, ref, ref, to_sib)

        def start(self):
            self.ring.start()
            self.give(0, self.whole(t))

        def forward(self):
            self.ring.forward()
            self.give(1, self.at(left, 1))
            self.give(2, self.at(right, 0))

        def near(self):
            self.ring.near()
            self.give(3, self.at(left, 0))
            self.give(4, self.at(right, 1))

        def last(self):
            self.ring.last()
            self.give(5, self.at(far, 1))
            self.give(6, self.at(far, 0))

        def sib_own(self):
            w.arrived(self.base, self.whole(sib), to_sib)

        def sib_near(self):
            other = 1 - 2 * c
            for k, (block, half) in enumerate(((left, 1), (right, 0), (left, 0), (right, 1))):
                w.arrived(self.base + 1 + k, self.at(block + other, half), to_sib)

        def sib_last(self):
            other = 1 - 2 * c
            w.arrived(self.base + 5, self.at(far + other, 1), to_sib)
            w.arrived(self.base + 6, self.at(far + other, 0), to_sib)

    ex_f = exchange(lambda to: send_f.at[to // 2], recv_f)
    qkv_rows = [RowGather(wq, k * width // 2, width // 2) for k in range(2)]
    qkv_rows[0].start()

    eye = (
        lax.broadcasted_iota(jnp.int32, (cap, cap), 0)
        == lax.broadcasted_iota(jnp.int32, (cap, cap), 1)
    )
    turned = lax.dot_general(
        jnp.where(eye, 1.0, 0.0).astype(F32), combine[...], NT,
        precision=lax.Precision.HIGHEST, preferred_element_type=F32,
    )
    for e in range(experts):
        wcol[e * cap:(e + 1) * cap, :] = turned[:, e:e + 1]

    padded = shards * cap
    lane = lax.broadcasted_iota(jnp.int32, (1, padded), 1)
    mine = s // 2
    offset = jnp.int32(0)
    offset_row = jnp.zeros((1, padded), jnp.int32)
    count_row = jnp.zeros((1, padded), jnp.int32)
    for shard in range(shards):
        count = counts[mine, shard]
        here = lane // cap == shard
        offset_row = jnp.where(here, offset, offset_row)
        count_row = jnp.where(here, count, count_row)
        offset = offset + count
    position = jnp.where(lane % cap < count_row, offset_row + lane % cap, -1)
    row_ids = lax.broadcasted_iota(jnp.int32, comp.shape, 0)
    comp[...] = jnp.where(row_ids == position, 1.0, 0.0).astype(BF)

    load_half.wait()
    for k in range(RING):
        part = slice(k * width, (k + 1) * width)
        taken = dot(sel[...], ups_half[:, part], TN) * wcol[...]
        send_b[:, :, part] = taken.astype(BF).reshape(experts, cap, width)

    other = 1 - 2 * c

    def win_at(j):
        return win[pl.ds(pl.multiple_of(j * width, width), width), :]

    def wout_at(j):
        return wout[:, pl.ds(pl.multiple_of(j * width, width), width)]

    def gathered(gather, weight_at, dims):
        buf = gather.buf

        def add(j, first=False):
            term = dot(buf[j], weight_at(j), dims)
            if first:
                acc[...] = term
            else:
                acc[...] += term

        add(t, True)
        gather.sib_own()
        add(sib)
        gather.near()
        add(left)
        add(right)
        gather.last()
        gather.sib_near()
        add(left + other)
        add(right + other)
        add(far)
        gather.sib_last()
        add(far + other)

    class RowReduce:
        def __init__(self, k):
            self.k = k
            self.base = w.take(10)

        def partials(self, lhs, weight_at, dims):
            k, b = self.k, self.base
            for d in (2, 1, 3, 0):
                j = wrap(x + d) * 2 + 1 - c
                pst[k, d] = dot(lhs[...], weight_at(j), dims).astype(BF)
                w.send(b + d, pst.at[k, d], d2d.at[k, d], to_sib)
            lo, hi = pl.ds(0, half_rows), pl.ds(half_rows, half_rows)
            for d in (2, 1, 3, 0):
                j = wrap(x + d) * 2 + c
                own = dot(lhs[...], weight_at(j), dims)
                w.arrived(b + d, d2d.at[k, d], to_sib)
                sbuf[k, d] = (own + d2d[k, d].astype(F32)).astype(BF)
                if d == 2:
                    w.send(b + 4, sbuf.at[k, d, hi], half_l.at[k], to_right)
                    w.send(b + 5, sbuf.at[k, d, lo], half_r.at[k], to_left)
                elif d == 1:
                    w.send(b + 6, sbuf.at[k, d, lo], full_l.at[k, lo], to_right)
                elif d == 3:
                    w.send(b + 7, sbuf.at[k, d, hi], full_r.at[k, hi], to_left)

        def forward(self):
            k, b = self.k, self.base
            lo, hi = pl.ds(0, half_rows), pl.ds(half_rows, half_rows)
            w.arrived(b + 4, half_l.at[k], to_right)
            sbuf[k, 1, hi] = (sbuf[k, 1, hi].astype(F32) + half_l[k].astype(F32)).astype(BF)
            w.send(b + 8, sbuf.at[k, 1, hi], full_l.at[k, hi], to_right)
            w.arrived(b + 5, half_r.at[k], to_left)
            sbuf[k, 3, lo] = (sbuf[k, 3, lo].astype(F32) + half_r[k].astype(F32)).astype(BF)
            w.send(b + 9, sbuf.at[k, 3, lo], full_r.at[k, lo], to_left)

        def result(self):
            k, b = self.k, self.base
            lo, hi = pl.ds(0, half_rows), pl.ds(half_rows, half_rows)
            w.arrived(b + 6, full_l.at[k, lo], to_right)
            w.arrived(b + 7, full_r.at[k, hi], to_left)
            w.arrived(b + 8, full_l.at[k, hi], to_right)
            w.arrived(b + 9, full_r.at[k, lo], to_left)
            total = sbuf[k, 0].astype(F32) + full_l[k].astype(F32) + full_r[k].astype(F32)
            return total.astype(BF)

    def send_back(k, rows):
        ret_s[k] = dot(comp[...], rows, TN).astype(BF).reshape(ret_s.shape[1:])
        return exchange(lambda to: ret_s.at[k, to], ret_r.at[k])

    def returned(k, base):
        exchanged(base, ret_r.at[k])
        pairs = ret_r[k].reshape(experts, 2, cap, width).astype(F32)
        return (pairs[:, 0] + pairs[:, 1]).reshape(slots, width)

    def scatter(values):
        high = values.astype(BF)
        low = (values - high.astype(F32)).astype(BF)
        return dot(sel[...], high) + dot(sel[...], low)

    gather_f = RowGather(ag_f, 0, n_tok)
    exchanged(ex_f, recv_f)
    ag_f[t] = dot(comp[...], recv_f[...].reshape(padded, width)).astype(BF)
    gather_f.start()
    ex_b = exchange(lambda to: send_b.at[to // 2], recv_b)
    gather_f.forward()
    qkv_rows[0].forward()
    load_win.wait()
    gathered(gather_f, win_at, NN)
    pre = acc[...]
    cdf = 0.5 * (1.0 + lax.erf(pre * 0.7071067811865476))
    hid[...] = (pre * cdf).astype(BF)
    slope[...] = cdf + pre * jnp.exp(-0.5 * pre * pre) * 0.3989422804014327
    load_wout.wait()
    reduce_f = RowReduce(0)
    reduce_f.partials(hid, wout_at, NN)


    reduce_f.forward()
    qkv_rows[0].near()
    qkv_rows[0].last()
    back_f = send_back(0, reduce_f.result())
    qkv_rows[1].start()

    give_b = w.take(RING)
    exchanged(ex_b, recv_b)
    for k in range(RING):
        part = recv_b[:, :, k * width:(k + 1) * width].reshape(padded, width)
        mine_k = ag_b.at[c * RING + k]
        mine_k[...] = dot(comp[...], part).astype(BF)
        w.send(give_b + k, mine_k, mine_k, to_sib)
    for k in range(2 * RING):
        j = c * RING + k if k < RING else (1 - c) * RING + k - RING
        if k >= RING:
            w.arrived(give_b + k - RING, ag_b.at[j], to_sib)
        term = dot(ag_b[j], wout_at(j), NT)
        if k == 0:
            acc[...] = term
        else:
            acc[...] += term
    pgr[...] = (acc[...] * slope[...]).astype(BF)
    halves = returned(0, back_f)
    mixture = scatter(halves * wcol[...])
    layer = (tok[...].astype(F32) + mixture).astype(BF)
    lay_s[...] = layer.reshape(lay_s.shape)
    line_base = w.take(parts)

    def to_line(i, carry):
        to = lax.rem(t + i, parts)
        w.send(line_base + i, lay_s.at[to], lay.at[z, y, t], (s, to), keep=False)
        return carry

    def from_line(i, carry):
        source = lax.rem(t - i + parts, parts)
        w.arrived(line_base + i, lay.at[z, y, source], (s, source))
        return carry

    def line_end(i, carry):
        w.copy(line_base + i, lay_s.at[0], lay_s.at[0], to_sib).wait_send()
        return carry

    lax.fori_loop(1, parts, to_line, 0)
    lay[z, y, t] = lay_s[t]
    qkv_rows[1].forward()

    reduce_b = RowReduce(1)
    reduce_b.partials(pgr, win_at, NT)
    lax.fori_loop(1, parts, from_line, 0)

    def along_y(part, zz):
        def at(pos, half):
            return lay.at[zz, pos, pl.ds(part * RING + half * 2, 2)]
        return RingGather(w, at, y, y_minus, y_plus, y_far, to_ym, to_yp)

    def along_z(part, yy):
        def at(pos, half):
            return lay.at[pos, yy, pl.ds(part * RING + half * 2, 2)]
        return RingGather(w, at, z, z_minus, z_plus, z_far, to_zm, to_zp)

    first_p, first_q = along_y(0, z), along_z(1, y)
    second_p = [along_z(0, yy) for yy in (y, y_minus, y_plus, y_far)]
    second_q = [along_y(1, zz) for zz in (z, z_minus, z_plus, z_far)]
    first_p.start()
    first_q.start()
    second_p[0].start()
    second_q[0].start()

    rows_of_four = RING * piece

    def products(blocks_at, first):
        total = None
        for k in range(first, first + RING):
            term = dot(blocks_at(k).reshape(rows_of_four, width), wq[k])
            total = term if total is None else total + term
        return total.reshape(RING, piece, -1)

    def group_p(zz):
        sum_p[zz] = products(lambda k: lay[zz, :, k], 0)

    def group_q(yy):
        sum_q[:, yy] = products(lambda k: lay[:, yy, k], RING)

    out_base = w.take(2 * parts)

    def out_copy(zz, yy):
        to = zz * 2 + yy // 2
        return to, pltpu.make_async_remote_copy(
            src_ref=out_s.at[zz, yy],
            dst_ref=projected.at[lax.rem(yy, 2), t],
            send_sem=send_sems.at[out_base + zz * RING + yy],
            recv_sem=recv_sems.at[out_base + lax.rem(yy, 2) * parts + t],
            device_id=(s, to),
            device_id_type=pl.DeviceIdType.MESH,
        )

    def deliver(zz, yy):
        out_s[zz, yy] = (sum_p[zz, yy] + sum_q[zz, yy]).astype(BF)
        to, copy = out_copy(zz, yy)

        @pl.when(to != t)
        def _():
            copy.start()

        @pl.when(to == t)
        def _():
            projected[lax.rem(yy, 2), t] = out_s[zz, yy]

    first_p.forward()
    first_q.forward()
    second_p[0].forward()
    second_q[0].forward()
    first_p.near()
    first_q.near()
    for k in (1, 2):
        second_p[k].start()
        second_q[k].start()
    reduce_b.forward()
    qkv_rows[1].near()
    qkv_rows[1].last()
    first_p.last()
    first_q.last()
    second_p[3].start()
    second_q[3].start()
    for k in (1, 2):
        second_p[k].forward()
        second_q[k].forward()
    for gather in qkv_rows:
        gather.sib_own()
        gather.sib_near()
        gather.sib_last()
    group_p(z)
    group_q(y)
    second_p[3].forward()
    second_q[3].forward()
    back_b = send_back(1, reduce_b.result())
    for j in range(parts):
        part = slice(j * width, (j + 1) * width)
        grad_in[part, :] = dot(ag_f[j], pgr[...], TN).astype(BF)
    for k in range(RING):
        second_p[k].near()
        second_q[k].near()
    group_p(z_plus)
    group_q(y_plus)
    group_p(z_minus)
    group_q(y_minus)
    for zz in (z_plus, z_minus, z):
        for yy in (y_plus, y_minus, y):
            deliver(zz, yy)
    hid_turned = hid[...].T
    for j in range(parts):
        part = slice(j * width, (j + 1) * width)
        grad_out[:, part] = dot(hid_turned, ag_b[j]).astype(BF)
    load_ups.wait()
    back_rows = scatter(returned(1, back_b))
    grad_tokens[...] = (ups[...].astype(F32) + back_rows).astype(BF)
    for k in range(RING):
        second_p[k].last()
    group_p(z_far)
    for yy in (y_plus, y_minus, y):
        deliver(z_far, yy)
    for k in range(RING):
        second_q[k].last()
    group_q(y_far)
    for zz in (z_far, z_plus, z_minus, z):
        deliver(zz, y_far)

    def out_end(i, carry):
        to, copy = out_copy(i // RING, lax.rem(i, RING))

        @pl.when(to != t)
        def _():
            copy.wait_send()

        return carry

    def out_arrived(i, carry):
        source = lax.rem(t - i + parts, parts)
        for shard in range(2):
            slot = out_base + shard * parts + source
            w.arrived(slot, projected.at[shard, source], (s, source))
        return carry

    lax.fori_loop(1, parts, out_arrived, 0)
    lax.fori_loop(0, shards, out_end, 0)
    lax.fori_loop(1, parts, line_end, 0)

    for copy in w.sent:
        copy.wait_send()
    exchange_end(ex_f, recv_f)
    exchange_end(ex_b, recv_b)
    exchange_end(back_f, ret_r.at[0])
    exchange_end(back_b, ret_r.at[1])


def write_kernel(
    grad_in_v, grad_out_v, products, grads, projected, grad_tokens, grad_in, grad_out, sems
):
    copies = []
    for src, dst in ((grad_in_v, grad_in.at[0]), (grad_out_v, grad_out.at[0]), (grads, grad_tokens)):
        copies.append(pltpu.make_async_copy(src, dst, sems.at[len(copies)]))
        copies[-1].start()
    blocks = products.shape[1] // 128
    turn = row_permutation(blocks, False)
    for f in range(0, products.shape[0], BAND):
        block = products[f:f + BAND, :]
        stacked = jnp.concatenate(
            [block[:, k * 128:(k + 1) * 128] for k in range(blocks)], axis=0
        )
        projected[f * blocks:(f + BAND) * blocks, :] = dot(turn, stacked).astype(BF)
    for copy in copies:
        copy.wait()


def on_device(tokens, picked, counts, combine, w_in, w_out, w_qkv, upstream):
    n_tok, width = tokens.shape
    experts, cap = picked.shape[0], picked.shape[2]
    parts, shards = 8, 16
    slice_w = width // parts
    rows = experts * cap
    hidden = w_in.shape[2]
    heads, kinds, lanes = w_qkv.shape[1:]
    columns = heads * kinds * lanes
    flat = w_qkv.transpose(0, 2, 1, 3).reshape(slice_w * kinds * heads, lanes)
    anywhere = pl.BlockSpec(memory_space=pl.ANY)
    vmem = pl.BlockSpec(memory_space=pltpu.VMEM)
    smem = pl.BlockSpec(memory_space=pltpu.SMEM)
    sems = 340
    out = pl.pallas_call(
        layer_kernel,
        out_shape=(
            pltpu.VMEM((2, parts, n_tok // parts, columns), BF),
            pltpu.VMEM((n_tok, slice_w), BF),
            pltpu.VMEM((width, hidden), BF),
            pltpu.VMEM((hidden, width), BF),
        ),
        in_specs=[anywhere] * 5 + [vmem, smem, vmem],
        out_specs=[vmem] * 4,
        scratch_shapes=[
            pltpu.VMEM((n_tok, slice_w), BF),
            pltpu.VMEM((n_tok, slice_w), BF),
            pltpu.VMEM((n_tok, width // 2), BF),
            pltpu.VMEM((width, hidden), BF),
            pltpu.VMEM((hidden, width), BF),
            pltpu.VMEM(flat.shape, BF),
            pltpu.VMEM((parts, slice_w, columns), BF),
            pltpu.VMEM((n_tok, rows), BF),
            pltpu.VMEM((rows, shards * cap), BF),
            pltpu.VMEM((rows, 1), F32),
            pltpu.VMEM((experts, cap, slice_w), BF),
            pltpu.VMEM((experts, cap, width // 2), BF),
            pltpu.VMEM((shards, cap, slice_w), BF),
            pltpu.VMEM((shards, cap, width // 2), BF),
            pltpu.VMEM((parts, rows, slice_w), BF),
            pltpu.VMEM((parts, rows, slice_w), BF),
            pltpu.VMEM((rows, hidden), F32),
            pltpu.VMEM((rows, hidden), F32),
            pltpu.VMEM((rows, hidden), BF),
            pltpu.VMEM((rows, hidden), BF),
            pltpu.VMEM((2, RING, rows, slice_w), BF),
            pltpu.VMEM((2, RING, rows, slice_w), BF),
            pltpu.VMEM((2, RING, rows, slice_w), BF),
            pltpu.VMEM((2, rows // 2, slice_w), BF),
            pltpu.VMEM((2, rows // 2, slice_w), BF),
            pltpu.VMEM((2, rows, slice_w), BF),
            pltpu.VMEM((2, rows, slice_w), BF),
            pltpu.VMEM((2, shards, cap, slice_w), BF),
            pltpu.VMEM((2, shards, cap, slice_w), BF),
            pltpu.VMEM((parts, n_tok // parts, slice_w), BF),
            pltpu.VMEM((RING, RING, parts, n_tok // parts, slice_w), BF),
            pltpu.VMEM((RING, RING, n_tok // parts, columns), F32),
            pltpu.VMEM((RING, RING, n_tok // parts, columns), F32),
            pltpu.VMEM((RING, RING, n_tok // parts, columns), BF),
            pltpu.SemaphoreType.DMA((6,)),
            pltpu.SemaphoreType.DMA((sems,)),
            pltpu.SemaphoreType.DMA((sems,)),
        ],
        compiler_params=pltpu.CompilerParams(
            collective_id=0, has_side_effects=True, vmem_limit_bytes=50 * 1024 * 1024
        ),
        cost_estimate=pl.CostEstimate(
            flops=8 * 10**9, bytes_accessed=20 * 10**6, transcendentals=3 * 10**5
        ),
        name="moe_layer",
    )(
        tokens, upstream, w_in, w_out, flat,
        picked[:, 0, :], counts, combine[:, 0, :],
    )
    products, grads, grad_in, grad_out = out
    projected, grad_tokens, grad_in, grad_out = pl.pallas_call(
        write_kernel,
        out_shape=(
            jax.ShapeDtypeStruct((2 * n_tok * kinds * heads, lanes), BF),
            jax.ShapeDtypeStruct((n_tok, slice_w), BF),
            jax.ShapeDtypeStruct(w_in.shape, BF),
            jax.ShapeDtypeStruct(w_out.shape, BF),
        ),
        in_specs=[vmem] * 4,
        out_specs=(vmem, anywhere, anywhere, anywhere),
        scratch_shapes=[pltpu.SemaphoreType.DMA((3,))],
        compiler_params=pltpu.CompilerParams(vmem_limit_bytes=16 * 1024 * 1024),
        cost_estimate=pl.CostEstimate(
            flops=2 * 10**8, bytes_accessed=18 * 10**6, transcendentals=0
        ),
        name="write_out",
    )(grad_in, grad_out, products.reshape(2 * n_tok, columns), grads)
    projected = projected.reshape(2 * n_tok, kinds, heads, lanes).transpose(0, 2, 1, 3)
    return projected, grad_tokens, grad_in, grad_out


def solution(mesh):
    return jax.shard_map(
        on_device,
        mesh=mesh,
        in_specs=(
            P("expert", None),
            P(None, "expert", None),
            P(),
            P(None, "expert", None),
            P("expert", None, "tensor"),
            P("expert", "tensor", None),
            P("tensor", "expert", None, None),
            P("expert", None),
        ),
        out_specs=(
            P("tensor", "expert", None, None),
            P("expert", "tensor"),
            P("expert", None, "tensor"),
            P("expert", "tensor", None),
        ),
        check_vma=False,
    )
```

```python
import jax
import jax.numpy as jnp
from jax import lax
from jax.experimental import pallas as pl
from jax.experimental.pallas import tpu as pltpu
from jax.sharding import PartitionSpec as P

BF = jnp.bfloat16
F32 = jnp.float32
NN = (((1,), (0,)), ((), ()))
NT = (((1,), (1,)), ((), ()))
TN = (((0,), (0,)), ((), ()))
RING = 4
BAND = 32
OFFSETS = sorted(
    ((dz, dy) for dz in range(RING) for dy in range(RING) if dz or dy),
    key=lambda step: -sum(min(d, RING - d) for d in step),
)


def dot(a, b, dims=NN):
    return lax.dot_general(a, b, dims, preferred_element_type=F32)


def row_permutation(blocks, gather):
    n = BAND * blocks
    a = lax.broadcasted_iota(jnp.int32, (n, n), 0)
    b = lax.broadcasted_iota(jnp.int32, (n, n), 1)
    if not gather:
        a, b = b, a
    return jnp.where((a % BAND) * blocks + a // BAND == b, 1.0, 0.0).astype(BF)


class Wires:
    def __init__(self, send_sems, recv_sems):
        self.send_sems, self.recv_sems = send_sems, recv_sems
        self.next = 0
        self.sent = []

    def take(self, count=1):
        first = self.next
        self.next += count
        return first

    def copy(self, slot, src, dst, device):
        return pltpu.make_async_remote_copy(
            src_ref=src,
            dst_ref=dst,
            send_sem=self.send_sems.at[slot],
            recv_sem=self.recv_sems.at[slot],
            device_id=device,
            device_id_type=pl.DeviceIdType.MESH,
        )

    def send(self, slot, src, dst, device, keep=True):
        copy = self.copy(slot, src, dst, device)
        copy.start()
        if keep:
            self.sent.append(copy)

    def arrived(self, slot, dst, device):
        self.copy(slot, dst, dst, device).wait_recv()


class RingGather:
    def __init__(self, wires, at, me, minus, plus, far, to_minus, to_plus):
        self.w, self.at = wires, at
        self.me, self.minus, self.plus, self.far = me, minus, plus, far
        self.to_minus, self.to_plus = to_minus, to_plus
        self.base = wires.take(6)

    def start(self, half):
        ref, b = self.at(self.me, half), self.base
        self.w.send(b + 1 - half, ref, ref, self.to_plus)
        self.w.send(b + 3 + half, ref, ref, self.to_minus)

    def forward(self, half):
        b = self.base
        if half:
            ref = self.at(self.minus, 1)
            self.w.arrived(b, ref, self.to_plus)
            self.w.send(b + 2, ref, ref, self.to_plus)
        else:
            ref = self.at(self.plus, 0)
            self.w.arrived(b + 3, ref, self.to_minus)
            self.w.send(b + 5, ref, ref, self.to_minus)

    def near(self, half):
        if half:
            self.w.arrived(self.base + 4, self.at(self.plus, 1), self.to_minus)
        else:
            self.w.arrived(self.base + 1, self.at(self.minus, 0), self.to_plus)

    def last(self, half):
        if half:
            self.w.arrived(self.base + 2, self.at(self.far, 1), self.to_plus)
        else:
            self.w.arrived(self.base + 5, self.at(self.far, 0), self.to_minus)


def layer_kernel(
    tokens, upstream, w_in, w_out, w_qkv, picked, counts, combine,
    projected, grad_tokens, grad_in, grad_out,
    tok, ups, ups_half, win, wout, wraw, wq, sel, comp, wcol,
    send_f, send_b, recv_f, recv_b, ag_f, ag_b,
    acc, slope, hid, pgr,
    pst, d2d, sbuf, half_l, half_r, full_l, full_r,
    ret_s, ret_r, lay_s, lay, sum_p, sum_q, out_s,
    load_sems, send_sems, recv_sems,
):
    s, t = lax.axis_index("expert"), lax.axis_index("tensor")
    z, y = s // RING, s % RING
    x, c = t // 2, t % 2
    shards, parts = RING * RING, 2 * RING
    experts, cap = counts.shape[0], combine.shape[1]
    n_tok, width = tok.shape
    half_rows = n_tok // 2
    piece = n_tok // parts

    def wrap(v):
        return lax.rem(v + RING, RING)

    left, right = wrap(x - 1) * 2 + c, wrap(x + 1) * 2 + c
    far = wrap(x + 2) * 2 + c
    sib = x * 2 + 1 - c
    to_left, to_right, to_sib = (s, left), (s, right), (s, sib)
    y_minus, y_plus, y_far = wrap(y - 1), wrap(y + 1), wrap(y + 2)
    z_minus, z_plus, z_far = wrap(z - 1), wrap(z + 1), wrap(z + 2)
    to_ym, to_yp = (z * RING + y_minus, t), (z * RING + y_plus, t)
    to_zm, to_zp = (z_minus * RING + y, t), (z_plus * RING + y, t)

    cols = pl.ds(pl.multiple_of(t * width, width), width)
    load_tok = pltpu.make_async_copy(tokens.at[:, cols], tok, load_sems.at[0])
    load_ups = pltpu.make_async_copy(upstream.at[:, cols], ups, load_sems.at[1])
    load_win = pltpu.make_async_copy(w_in.at[0], win, load_sems.at[2])
    load_wout = pltpu.make_async_copy(w_out.at[0], wout, load_sems.at[3])
    wide_cols = pl.ds(pl.multiple_of(c * RING * width, width), RING * width)
    load_half = pltpu.make_async_copy(upstream.at[:, wide_cols], ups_half, load_sems.at[4])
    load_qkv = pltpu.make_async_copy(w_qkv, wraw, load_sems.at[5])
    load_tok.start()
    barrier = pltpu.get_barrier_semaphore()

    def greet(i, carry):
        pl.semaphore_signal(
            barrier, inc=1, device_id=(lax.rem(s + i, shards), t),
            device_id_type=pl.DeviceIdType.MESH,
        )
        return carry

    lax.fori_loop(1, shards, greet, 0)

    def greet_line(i, carry):
        pl.semaphore_signal(
            barrier, inc=1, device_id=(s, lax.rem(t + i, parts)),
            device_id_type=pl.DeviceIdType.MESH,
        )
        return carry

    lax.fori_loop(1, parts, greet_line, 0)

    load_half.start()
    load_win.start()
    load_wout.start()
    load_qkv.start()
    load_ups.start()

    slots = experts * cap
    lane = lax.broadcasted_iota(jnp.int32, (1, slots), 1)
    spread = (
        lax.broadcasted_iota(jnp.int32, (cap, slots), 1) % cap
        == lax.broadcasted_iota(jnp.int32, (cap, slots), 0)
    )
    spread = jnp.where(spread, 1.0, 0.0).astype(BF)
    wide = dot(picked[...].astype(F32).astype(BF), spread)
    own_row = (
        lax.broadcasted_iota(jnp.int32, (experts, slots), 1) // cap
        == lax.broadcasted_iota(jnp.int32, (experts, slots), 0)
    )
    pick_row = jnp.sum(jnp.where(own_row, wide, 0.0), axis=0, keepdims=True).astype(jnp.int32)
    count_row = jnp.zeros((1, slots), jnp.int32)
    for e in range(experts):
        count_row = jnp.where(lane // cap == e, counts[e, s], count_row)
    pick_row = jnp.where(lane % cap < count_row, pick_row, -1)
    token_ids = lax.broadcasted_iota(jnp.int32, (n_tok, slots), 0)
    sel[...] = jnp.where(token_ids == pick_row, 1.0, 0.0).astype(BF)

    load_tok.wait()
    send_f[...] = dot(sel[...], tok[...], TN).astype(BF).reshape(send_f.shape)

    pl.semaphore_wait(barrier, shards - 1 + parts - 1)

    w = Wires(send_sems, recv_sems)

    def exchange(src_at, recv):
        base = w.take(shards)

        for dz, dy in OFFSETS:
            to = wrap(z + dz) * RING + wrap(y + dy)
            w.send(base + dz * RING + dy, src_at(to), recv.at[s], (to, t), keep=False)
        recv[s] = src_at(s)[...]
        return base

    def exchanged(base, recv):
        for dz, dy in OFFSETS:
            source = wrap(z - dz) * RING + wrap(y - dy)
            w.arrived(base + dz * RING + dy, recv.at[source], (source, t))

    def exchange_end(base, recv):
        def body(i, carry):
            w.copy(base + i, recv.at[0], recv.at[0], to_sib).wait_send()
            return carry

        lax.fori_loop(1, shards, body, 0)

    class RowGather:
        def __init__(self, buf, first, count):
            self.buf = buf
            self.whole = lambda block: buf.at[block, pl.ds(first, count), :]

            def at(block, half):
                return buf.at[block, pl.ds(first + half * count // 2, count // 2), :]

            self.ring = RingGather(w, at, t, left, right, far, to_left, to_right)
            self.base = w.take(7)
            self.at = at

        def give(self, k, ref):
            w.send(self.base + k, ref, ref, to_sib)

        def start(self):
            self.ring.start(1)
            self.ring.start(0)
            self.give(0, self.whole(t))

        def forward(self):
            self.ring.forward(1)
            self.ring.forward(0)
            self.give(1, self.at(left, 1))
            self.give(2, self.at(right, 0))

        def near(self):
            self.ring.near(0)
            self.ring.near(1)
            self.give(3, self.at(left, 0))
            self.give(4, self.at(right, 1))

        def last(self):
            self.ring.last(1)
            self.ring.last(0)
            self.give(5, self.at(far, 1))
            self.give(6, self.at(far, 0))

        def sib_own(self):
            w.arrived(self.base, self.whole(sib), to_sib)

        def sib_near(self):
            other = 1 - 2 * c
            for k, (block, half) in enumerate(((left, 1), (right, 0), (left, 0), (right, 1))):
                w.arrived(self.base + 1 + k, self.at(block + other, half), to_sib)

        def sib_last(self):
            other = 1 - 2 * c
            w.arrived(self.base + 5, self.at(far + other, 1), to_sib)
            w.arrived(self.base + 6, self.at(far + other, 0), to_sib)

    ex_f = exchange(lambda to: send_f.at[to // 2], recv_f)
    part_rows = (5 * width // 16, 6 * width // 16, 5 * width // 16)
    qkv_rows = [RowGather(wq, sum(part_rows[:k]), n) for k, n in enumerate(part_rows)]
    load_qkv.wait()
    blocks = wq.shape[2] // 128
    turn = row_permutation(blocks, True)
    for f in range(0, width, BAND):
        moved = dot(turn, wraw[f * blocks:(f + BAND) * blocks, :]).astype(BF)
        for k in range(blocks):
            wq[t, f:f + BAND, k * 128:(k + 1) * 128] = moved[k * BAND:(k + 1) * BAND]

    qkv_rows[0].start()

    eye = (
        lax.broadcasted_iota(jnp.int32, (cap, cap), 0)
        == lax.broadcasted_iota(jnp.int32, (cap, cap), 1)
    )
    turned = lax.dot_general(
        jnp.where(eye, 1.0, 0.0).astype(F32), combine[...], NT,
        precision=lax.Precision.HIGHEST, preferred_element_type=F32,
    )
    for e in range(experts):
        wcol[e * cap:(e + 1) * cap, :] = turned[:, e:e + 1]

    padded = shards * cap
    lane = lax.broadcasted_iota(jnp.int32, (1, padded), 1)
    mine = s // 2
    offset = jnp.int32(0)
    offset_row = jnp.zeros((1, padded), jnp.int32)
    count_row = jnp.zeros((1, padded), jnp.int32)
    for shard in range(shards):
        count = counts[mine, shard]
        here = lane // cap == shard
        offset_row = jnp.where(here, offset, offset_row)
        count_row = jnp.where(here, count, count_row)
        offset = offset + count
    position = jnp.where(lane % cap < count_row, offset_row + lane % cap, -1)
    row_ids = lax.broadcasted_iota(jnp.int32, comp.shape, 0)
    comp[...] = jnp.where(row_ids == position, 1.0, 0.0).astype(BF)

    load_half.wait()
    for k in range(RING):
        part = slice(k * width, (k + 1) * width)
        taken = dot(sel[...], ups_half[:, part], TN) * wcol[...]
        send_b[:, :, part] = taken.astype(BF).reshape(experts, cap, width)

    other = 1 - 2 * c

    def win_at(j):
        return win[pl.ds(pl.multiple_of(j * width, width), width), :]

    def wout_at(j):
        return wout[:, pl.ds(pl.multiple_of(j * width, width), width)]

    def gathered(gather, weight_at, dims):
        buf = gather.buf

        def add(j, first=False):
            term = dot(buf[j], weight_at(j), dims)
            if first:
                acc[...] = term
            else:
                acc[...] += term

        add(t, True)
        gather.sib_own()
        add(sib)
        gather.near()
        add(left)
        add(right)
        gather.last()
        gather.sib_near()
        add(left + other)
        add(right + other)
        add(far)
        gather.sib_last()
        add(far + other)

    class RowReduce:
        def __init__(self, k):
            self.k = k
            self.base = w.take(10)

        def partials(self, lhs, weight_at, dims):
            k, b = self.k, self.base
            for d in (2, 1, 3, 0):
                j = wrap(x + d) * 2 + 1 - c
                pst[k, d] = dot(lhs[...], weight_at(j), dims).astype(BF)
                w.send(b + d, pst.at[k, d], d2d.at[k, d], to_sib)
            lo, hi = pl.ds(0, half_rows), pl.ds(half_rows, half_rows)
            for d in (2, 1, 3, 0):
                j = wrap(x + d) * 2 + c
                own = dot(lhs[...], weight_at(j), dims)
                w.arrived(b + d, d2d.at[k, d], to_sib)
                sbuf[k, d] = (own + d2d[k, d].astype(F32)).astype(BF)
                if d == 2:
                    w.send(b + 4, sbuf.at[k, d, hi], half_l.at[k], to_right)
                    w.send(b + 5, sbuf.at[k, d, lo], half_r.at[k], to_left)
                elif d == 1:
                    w.send(b + 6, sbuf.at[k, d, lo], full_l.at[k, lo], to_right)
                elif d == 3:
                    w.send(b + 7, sbuf.at[k, d, hi], full_r.at[k, hi], to_left)

        def forward(self):
            k, b = self.k, self.base
            lo, hi = pl.ds(0, half_rows), pl.ds(half_rows, half_rows)
            w.arrived(b + 4, half_l.at[k], to_right)
            sbuf[k, 1, hi] = (sbuf[k, 1, hi].astype(F32) + half_l[k].astype(F32)).astype(BF)
            w.send(b + 8, sbuf.at[k, 1, hi], full_l.at[k, hi], to_right)
            w.arrived(b + 5, half_r.at[k], to_left)
            sbuf[k, 3, lo] = (sbuf[k, 3, lo].astype(F32) + half_r[k].astype(F32)).astype(BF)
            w.send(b + 9, sbuf.at[k, 3, lo], full_r.at[k, lo], to_left)

        def result(self):
            k, b = self.k, self.base
            lo, hi = pl.ds(0, half_rows), pl.ds(half_rows, half_rows)
            w.arrived(b + 6, full_l.at[k, lo], to_right)
            w.arrived(b + 7, full_r.at[k, hi], to_left)
            w.arrived(b + 8, full_l.at[k, hi], to_right)
            w.arrived(b + 9, full_r.at[k, lo], to_left)
            total = sbuf[k, 0].astype(F32) + full_l[k].astype(F32) + full_r[k].astype(F32)
            return total.astype(BF)

    def send_back(k, rows):
        ret_s[k] = dot(comp[...], rows, TN).astype(BF).reshape(ret_s.shape[1:])
        return exchange(lambda to: ret_s.at[k, to], ret_r.at[k])

    def returned(k, base):
        exchanged(base, ret_r.at[k])
        pairs = ret_r[k].reshape(experts, 2, cap, width).astype(F32)
        return (pairs[:, 0] + pairs[:, 1]).reshape(slots, width)

    def scatter(values):
        high = values.astype(BF)
        low = (values - high.astype(F32)).astype(BF)
        return dot(sel[...], high) + dot(sel[...], low)

    gather_f = RowGather(ag_f, 0, n_tok)
    exchanged(ex_f, recv_f)
    ag_f[t] = dot(comp[...], recv_f[...].reshape(padded, width)).astype(BF)
    gather_f.start()
    ex_b = exchange(lambda to: send_b.at[to // 2], recv_b)
    gather_f.forward()
    qkv_rows[0].forward()
    load_win.wait()
    gathered(gather_f, win_at, NN)
    pre = acc[...]
    cdf = 0.5 * (1.0 + lax.erf(pre * 0.7071067811865476))
    hid[...] = (pre * cdf).astype(BF)
    slope[...] = cdf + pre * jnp.exp(-0.5 * pre * pre) * 0.3989422804014327
    load_wout.wait()
    reduce_f = RowReduce(0)
    reduce_f.partials(hid, wout_at, NN)


    reduce_f.forward()
    qkv_rows[0].near()
    qkv_rows[0].last()
    back_f = send_back(0, reduce_f.result())
    qkv_rows[1].start()

    give_b = w.take(RING)
    exchanged(ex_b, recv_b)
    for k in range(RING):
        part = recv_b[:, :, k * width:(k + 1) * width].reshape(padded, width)
        mine_k = ag_b.at[c * RING + k]
        mine_k[...] = dot(comp[...], part).astype(BF)
        w.send(give_b + k, mine_k, mine_k, to_sib)
    for k in range(2 * RING):
        j = c * RING + k if k < RING else (1 - c) * RING + k - RING
        if k >= RING:
            w.arrived(give_b + k - RING, ag_b.at[j], to_sib)
        term = dot(ag_b[j], wout_at(j), NT)
        if k == 0:
            acc[...] = term
        else:
            acc[...] += term
    pgr[...] = (acc[...] * slope[...]).astype(BF)
    halves = returned(0, back_f)
    mixture = scatter(halves * wcol[...])
    layer = (tok[...].astype(F32) + mixture).astype(BF)
    lay_s[...] = layer.reshape(lay_s.shape)
    line_base = w.take(parts)

    def to_line(i, carry):
        to = lax.rem(t + i, parts)
        w.send(line_base + i, lay_s.at[to], lay.at[z, y, t], (s, to), keep=False)
        return carry

    def line_end(i, carry):
        w.copy(line_base + i, lay_s.at[0], lay_s.at[0], to_sib).wait_send()
        return carry

    lax.fori_loop(1, parts, to_line, 0)
    lay[z, y, t] = lay_s[t]

    def from_chip(chip):
        for core in range(2):
            source = chip * 2 + core
            w.arrived(
                line_base + lax.rem(t - source + parts, parts), lay.at[z, y, source], (s, source)
            )

    chips = ((x, wrap(x + 2)), (wrap(x + 1), wrap(x - 1)))

    def along_y(part, zz):
        def at(pos, half):
            return lay.at[zz, pos, pl.ds(chips[part][half] * 2, 2)]
        return RingGather(w, at, y, y_minus, y_plus, y_far, to_ym, to_yp)

    def along_z(part, yy):
        def at(pos, half):
            return lay.at[pos, yy, pl.ds(chips[part][half] * 2, 2)]
        return RingGather(w, at, z, z_minus, z_plus, z_far, to_zm, to_zp)

    first_p, first_q = along_y(0, z), along_z(1, y)
    second_p = [along_z(0, yy) for yy in (y, y_minus, y_plus, y_far)]
    second_q = [along_y(1, zz) for zz in (z, z_minus, z_plus, z_far)]
    w.arrived(line_base + lax.rem(t - sib + parts, parts), lay.at[z, y, sib], to_sib)
    first_p.start(0)
    second_p[0].start(0)
    reduce_b = RowReduce(1)
    reduce_b.partials(pgr, win_at, NT)
    for half in (0, 1):
        from_chip(chips[1][half])
        first_q.start(half)
        second_q[0].start(half)
    from_chip(chips[0][1])
    first_p.start(1)
    second_p[0].start(1)

    rows_of_four = RING * piece

    def products(blocks_at, part):
        total = None
        for half in range(2):
            for core in range(2):
                k = chips[part][half] * 2 + core
                term = dot(blocks_at(k).reshape(rows_of_four, width), wq[k])
                total = term if total is None else total + term
        return total.reshape(RING, piece, -1)

    def group_p(zz):
        sum_p[zz] = products(lambda k: lay[zz, :, k], 0)

    def group_q(yy):
        sum_q[:, yy] = products(lambda k: lay[:, yy, k], 1)

    out_base = w.take(2 * parts)

    def out_copy(zz, yy):
        to = zz * 2 + yy // 2
        return to, pltpu.make_async_remote_copy(
            src_ref=out_s.at[zz, yy],
            dst_ref=projected.at[lax.rem(yy, 2), t],
            send_sem=send_sems.at[out_base + zz * RING + yy],
            recv_sem=recv_sems.at[out_base + lax.rem(yy, 2) * parts + t],
            device_id=(s, to),
            device_id_type=pl.DeviceIdType.MESH,
        )

    def deliver(zz, yy):
        out_s[zz, yy] = (sum_p[zz, yy] + sum_q[zz, yy]).astype(BF)
        to, copy = out_copy(zz, yy)

        @pl.when(to != t)
        def _():
            copy.start()

        @pl.when(to == t)
        def _():
            projected[lax.rem(yy, 2), t] = out_s[zz, yy]

    first_p.forward(0)
    second_p[0].forward(0)
    first_p.near(0)
    for k in (1, 2):
        second_p[k].start(0)
    qkv_rows[1].forward()
    qkv_rows[2].start()
    for half in (0, 1):
        first_q.forward(half)
        second_q[0].forward(half)
    for half in (0, 1):
        first_q.near(half)
        for k in (1, 2):
            second_q[k].start(half)
    first_p.forward(1)
    second_p[0].forward(1)
    first_p.near(1)
    first_p.last(0)
    for k in (1, 2):
        second_p[k].start(1)
    second_p[3].start(0)
    for k in (1, 2):
        second_p[k].forward(0)
    for half in (0, 1):
        first_q.last(half)
        second_q[3].start(half)
    first_p.last(1)
    second_p[3].start(1)
    reduce_b.forward()
    for k in (1, 2):
        for half in (0, 1):
            second_q[k].forward(half)
        second_p[k].forward(1)
    qkv_rows[2].forward()
    second_p[3].forward(0)
    for half in (0, 1):
        second_q[3].forward(half)
    second_p[3].forward(1)
    for gather in qkv_rows[1:]:
        gather.near()
        gather.last()
    back_b = send_back(1, reduce_b.result())
    for gather in qkv_rows:
        gather.sib_own()
        gather.sib_near()
        gather.sib_last()
    group_p(z)
    group_q(y)
    deliver(z, y)
    for k in range(RING):
        for half in (0, 1):
            second_p[k].near(half)
            second_q[k].near(half)
    group_p(z_plus)
    group_p(z_minus)
    deliver(z_plus, y)
    deliver(z_minus, y)
    group_q(y_plus)
    group_q(y_minus)
    for zz in (z_plus, z_minus, z):
        for yy in (y_plus, y_minus):
            deliver(zz, yy)
    for k in range(RING):
        second_p[k].last(0)
        second_p[k].last(1)
    group_p(z_far)
    for yy in (y_plus, y_minus, y):
        deliver(z_far, yy)
    for k in range(RING):
        second_q[k].last(0)
        second_q[k].last(1)
    group_q(y_far)
    for zz in (z_far, z_plus, z_minus, z):
        deliver(zz, y_far)

    hid_turned = hid[...].T
    for j in range(parts):
        part = slice(j * width, (j + 1) * width)
        grad_in[part, :] = dot(ag_f[j], pgr[...], TN).astype(BF)
        grad_out[:, part] = dot(hid_turned, ag_b[j]).astype(BF)
    load_ups.wait()
    back_rows = scatter(returned(1, back_b))
    grad_tokens[...] = (ups[...].astype(F32) + back_rows).astype(BF)

    def out_end(i, carry):
        to, copy = out_copy(i // RING, lax.rem(i, RING))

        @pl.when(to != t)
        def _():
            copy.wait_send()

        return carry

    def out_arrived(i, carry):
        source = lax.rem(t - i + parts, parts)
        for shard in range(2):
            slot = out_base + shard * parts + source
            w.arrived(slot, projected.at[shard, source], (s, source))
        return carry

    lax.fori_loop(1, parts, out_arrived, 0)
    lax.fori_loop(0, shards, out_end, 0)
    lax.fori_loop(1, parts, line_end, 0)

    for copy in w.sent:
        copy.wait_send()
    exchange_end(ex_f, recv_f)
    exchange_end(ex_b, recv_b)
    exchange_end(back_f, ret_r.at[0])
    exchange_end(back_b, ret_r.at[1])


def write_kernel(
    grad_in_v, grad_out_v, products, grads, projected, grad_tokens, grad_in, grad_out, sems
):
    copies = []
    for src, dst in ((grad_in_v, grad_in.at[0]), (grad_out_v, grad_out.at[0]), (grads, grad_tokens)):
        copies.append(pltpu.make_async_copy(src, dst, sems.at[len(copies)]))
        copies[-1].start()
    blocks = products.shape[1] // 128
    turn = row_permutation(blocks, False)
    for f in range(0, products.shape[0], BAND):
        block = products[f:f + BAND, :]
        stacked = jnp.concatenate(
            [block[:, k * 128:(k + 1) * 128] for k in range(blocks)], axis=0
        )
        projected[f * blocks:(f + BAND) * blocks, :] = dot(turn, stacked).astype(BF)
    for copy in copies:
        copy.wait()


def on_device(tokens, picked, counts, combine, w_in, w_out, w_qkv, upstream):
    n_tok, width = tokens.shape
    experts, cap = picked.shape[0], picked.shape[2]
    parts, shards = 8, 16
    slice_w = width // parts
    rows = experts * cap
    hidden = w_in.shape[2]
    heads, kinds, lanes = w_qkv.shape[1:]
    columns = heads * kinds * lanes
    flat = w_qkv.transpose(0, 2, 1, 3).reshape(slice_w * kinds * heads, lanes)
    anywhere = pl.BlockSpec(memory_space=pl.ANY)
    vmem = pl.BlockSpec(memory_space=pltpu.VMEM)
    smem = pl.BlockSpec(memory_space=pltpu.SMEM)
    sems = 340
    out = pl.pallas_call(
        layer_kernel,
        out_shape=(
            pltpu.VMEM((2, parts, n_tok // parts, columns), BF),
            pltpu.VMEM((n_tok, slice_w), BF),
            pltpu.VMEM((width, hidden), BF),
            pltpu.VMEM((hidden, width), BF),
        ),
        in_specs=[anywhere] * 5 + [vmem, smem, vmem],
        out_specs=[vmem] * 4,
        scratch_shapes=[
            pltpu.VMEM((n_tok, slice_w), BF),
            pltpu.VMEM((n_tok, slice_w), BF),
            pltpu.VMEM((n_tok, width // 2), BF),
            pltpu.VMEM((width, hidden), BF),
            pltpu.VMEM((hidden, width), BF),
            pltpu.VMEM(flat.shape, BF),
            pltpu.VMEM((parts, slice_w, columns), BF),
            pltpu.VMEM((n_tok, rows), BF),
            pltpu.VMEM((rows, shards * cap), BF),
            pltpu.VMEM((rows, 1), F32),
            pltpu.VMEM((experts, cap, slice_w), BF),
            pltpu.VMEM((experts, cap, width // 2), BF),
            pltpu.VMEM((shards, cap, slice_w), BF),
            pltpu.VMEM((shards, cap, width // 2), BF),
            pltpu.VMEM((parts, rows, slice_w), BF),
            pltpu.VMEM((parts, rows, slice_w), BF),
            pltpu.VMEM((rows, hidden), F32),
            pltpu.VMEM((rows, hidden), F32),
            pltpu.VMEM((rows, hidden), BF),
            pltpu.VMEM((rows, hidden), BF),
            pltpu.VMEM((2, RING, rows, slice_w), BF),
            pltpu.VMEM((2, RING, rows, slice_w), BF),
            pltpu.VMEM((2, RING, rows, slice_w), BF),
            pltpu.VMEM((2, rows // 2, slice_w), BF),
            pltpu.VMEM((2, rows // 2, slice_w), BF),
            pltpu.VMEM((2, rows, slice_w), BF),
            pltpu.VMEM((2, rows, slice_w), BF),
            pltpu.VMEM((2, shards, cap, slice_w), BF),
            pltpu.VMEM((2, shards, cap, slice_w), BF),
            pltpu.VMEM((parts, n_tok // parts, slice_w), BF),
            pltpu.VMEM((RING, RING, parts, n_tok // parts, slice_w), BF),
            pltpu.VMEM((RING, RING, n_tok // parts, columns), F32),
            pltpu.VMEM((RING, RING, n_tok // parts, columns), F32),
            pltpu.VMEM((RING, RING, n_tok // parts, columns), BF),
            pltpu.SemaphoreType.DMA((6,)),
            pltpu.SemaphoreType.DMA((sems,)),
            pltpu.SemaphoreType.DMA((sems,)),
        ],
        compiler_params=pltpu.CompilerParams(
            collective_id=0, has_side_effects=True, vmem_limit_bytes=50 * 1024 * 1024
        ),
        cost_estimate=pl.CostEstimate(
            flops=8 * 10**9, bytes_accessed=20 * 10**6, transcendentals=3 * 10**5
        ),
        name="moe_layer",
    )(
        tokens, upstream, w_in, w_out, flat,
        picked[:, 0, :], counts, combine[:, 0, :],
    )
    products, grads, grad_in, grad_out = out
    projected, grad_tokens, grad_in, grad_out = pl.pallas_call(
        write_kernel,
        out_shape=(
            jax.ShapeDtypeStruct((2 * n_tok * kinds * heads, lanes), BF),
            jax.ShapeDtypeStruct((n_tok, slice_w), BF),
            jax.ShapeDtypeStruct(w_in.shape, BF),
            jax.ShapeDtypeStruct(w_out.shape, BF),
        ),
        in_specs=[vmem] * 4,
        out_specs=(vmem, anywhere, anywhere, anywhere),
        scratch_shapes=[pltpu.SemaphoreType.DMA((3,))],
        compiler_params=pltpu.CompilerParams(vmem_limit_bytes=16 * 1024 * 1024),
        cost_estimate=pl.CostEstimate(
            flops=2 * 10**8, bytes_accessed=18 * 10**6, transcendentals=0
        ),
        name="write_out",
    )(grad_in, grad_out, products.reshape(2 * n_tok, columns), grads)
    projected = projected.reshape(2 * n_tok, kinds, heads, lanes).transpose(0, 2, 1, 3)
    return projected, grad_tokens, grad_in, grad_out


def solution(mesh):
    return jax.shard_map(
        on_device,
        mesh=mesh,
        in_specs=(
            P("expert", None),
            P(None, "expert", None),
            P(),
            P(None, "expert", None),
            P("expert", None, "tensor"),
            P("expert", "tensor", None),
            P("tensor", "expert", None, None),
            P("expert", None),
        ),
        out_specs=(
            P("tensor", "expert", None, None),
            P("expert", "tensor"),
            P("expert", None, "tensor"),
            P("expert", "tensor", None),
        ),
        check_vma=False,
    )
```

```python
import jax
import jax.numpy as jnp
from jax import lax
from jax.experimental import pallas as pl
from jax.experimental.pallas import tpu as pltpu
from jax.sharding import PartitionSpec as P

BF = jnp.bfloat16
F32 = jnp.float32
NN = (((1,), (0,)), ((), ()))
NT = (((1,), (1,)), ((), ()))
TN = (((0,), (0,)), ((), ()))
RING = 4
BAND = 32
OFFSETS = sorted(
    ((dz, dy) for dz in range(RING) for dy in range(RING) if dz or dy),
    key=lambda step: -sum(min(d, RING - d) for d in step),
)


def dot(a, b, dims=NN):
    return lax.dot_general(a, b, dims, preferred_element_type=F32)


def row_permutation(blocks, gather):
    n = BAND * blocks
    a = lax.broadcasted_iota(jnp.int32, (n, n), 0)
    b = lax.broadcasted_iota(jnp.int32, (n, n), 1)
    if not gather:
        a, b = b, a
    return jnp.where((a % BAND) * blocks + a // BAND == b, 1.0, 0.0).astype(BF)


class Wires:
    def __init__(self, send_sems, recv_sems):
        self.send_sems, self.recv_sems = send_sems, recv_sems
        self.next = 0
        self.sent = []

    def take(self, count=1):
        first = self.next
        self.next += count
        return first

    def copy(self, slot, src, dst, device):
        return pltpu.make_async_remote_copy(
            src_ref=src,
            dst_ref=dst,
            send_sem=self.send_sems.at[slot],
            recv_sem=self.recv_sems.at[slot],
            device_id=device,
            device_id_type=pl.DeviceIdType.MESH,
        )

    def send(self, slot, src, dst, device, keep=True):
        copy = self.copy(slot, src, dst, device)
        copy.start()
        if keep:
            self.sent.append(copy)

    def arrived(self, slot, dst, device):
        self.copy(slot, dst, dst, device).wait_recv()


class RingGather:
    def __init__(self, wires, at, me, minus, plus, far, to_minus, to_plus):
        self.w, self.at = wires, at
        self.me, self.minus, self.plus, self.far = me, minus, plus, far
        self.to_minus, self.to_plus = to_minus, to_plus
        self.base = wires.take(6)

    def start(self, half):
        ref, b = self.at(self.me, half), self.base
        self.w.send(b + 1 - half, ref, ref, self.to_plus)
        self.w.send(b + 3 + half, ref, ref, self.to_minus)

    def forward(self, half):
        b = self.base
        if half:
            ref = self.at(self.minus, 1)
            self.w.arrived(b, ref, self.to_plus)
            self.w.send(b + 2, ref, ref, self.to_plus)
        else:
            ref = self.at(self.plus, 0)
            self.w.arrived(b + 3, ref, self.to_minus)
            self.w.send(b + 5, ref, ref, self.to_minus)

    def near(self, half):
        if half:
            self.w.arrived(self.base + 4, self.at(self.plus, 1), self.to_minus)
        else:
            self.w.arrived(self.base + 1, self.at(self.minus, 0), self.to_plus)

    def last(self, half):
        if half:
            self.w.arrived(self.base + 2, self.at(self.far, 1), self.to_plus)
        else:
            self.w.arrived(self.base + 5, self.at(self.far, 0), self.to_minus)


def layer_kernel(
    tokens, upstream, w_in, w_out, w_qkv, picked, counts, combine,
    projected, grad_tokens, grad_in, grad_out,
    tok, ups, ups_half, win, wout, wraw, wq, sel, comp, wcol,
    send_f, send_b, recv_f, recv_b, ag_f, ag_b,
    acc, slope, hid, pgr,
    pst, d2d, sbuf, half_l, half_r, full_l, full_r,
    ret_s, ret_r, lay_s, lay, sum_p, sum_q, out_s,
    load_sems, send_sems, recv_sems,
):
    s, t = lax.axis_index("expert"), lax.axis_index("tensor")
    z, y = s // RING, s % RING
    x, c = t // 2, t % 2
    shards, parts = RING * RING, 2 * RING
    experts, cap = counts.shape[0], combine.shape[1]
    n_tok, width = tok.shape
    half_rows = n_tok // 2
    piece = n_tok // parts

    def wrap(v):
        return lax.rem(v + RING, RING)

    left, right = wrap(x - 1) * 2 + c, wrap(x + 1) * 2 + c
    far = wrap(x + 2) * 2 + c
    sib = x * 2 + 1 - c
    to_left, to_right, to_sib = (s, left), (s, right), (s, sib)
    y_minus, y_plus, y_far = wrap(y - 1), wrap(y + 1), wrap(y + 2)
    z_minus, z_plus, z_far = wrap(z - 1), wrap(z + 1), wrap(z + 2)
    to_ym, to_yp = (z * RING + y_minus, t), (z * RING + y_plus, t)
    to_zm, to_zp = (z_minus * RING + y, t), (z_plus * RING + y, t)

    cols = pl.ds(pl.multiple_of(t * width, width), width)
    load_tok = pltpu.make_async_copy(tokens.at[:, cols], tok, load_sems.at[0])
    load_ups = pltpu.make_async_copy(upstream.at[:, cols], ups, load_sems.at[1])
    load_win = pltpu.make_async_copy(w_in.at[0], win, load_sems.at[2])
    load_wout = pltpu.make_async_copy(w_out.at[0], wout, load_sems.at[3])
    wide_cols = pl.ds(pl.multiple_of(c * RING * width, width), RING * width)
    load_half = pltpu.make_async_copy(upstream.at[:, wide_cols], ups_half, load_sems.at[4])
    load_qkv = pltpu.make_async_copy(w_qkv, wraw, load_sems.at[5])
    load_tok.start()
    barrier = pltpu.get_barrier_semaphore()

    def greet(i, carry):
        pl.semaphore_signal(
            barrier, inc=1, device_id=(lax.rem(s + i, shards), t),
            device_id_type=pl.DeviceIdType.MESH,
        )
        return carry

    lax.fori_loop(1, shards, greet, 0)

    def greet_line(i, carry):
        pl.semaphore_signal(
            barrier, inc=1, device_id=(s, lax.rem(t + i, parts)),
            device_id_type=pl.DeviceIdType.MESH,
        )
        return carry

    lax.fori_loop(1, parts, greet_line, 0)

    load_half.start()
    load_win.start()
    load_wout.start()
    load_qkv.start()
    load_ups.start()

    slots = experts * cap
    lane = lax.broadcasted_iota(jnp.int32, (1, slots), 1)
    spread = (
        lax.broadcasted_iota(jnp.int32, (cap, slots), 1) % cap
        == lax.broadcasted_iota(jnp.int32, (cap, slots), 0)
    )
    spread = jnp.where(spread, 1.0, 0.0).astype(BF)
    wide = dot(picked[...].astype(F32).astype(BF), spread)
    own_row = (
        lax.broadcasted_iota(jnp.int32, (experts, slots), 1) // cap
        == lax.broadcasted_iota(jnp.int32, (experts, slots), 0)
    )
    pick_row = jnp.sum(jnp.where(own_row, wide, 0.0), axis=0, keepdims=True).astype(jnp.int32)
    count_row = jnp.zeros((1, slots), jnp.int32)
    for e in range(experts):
        count_row = jnp.where(lane // cap == e, counts[e, s], count_row)
    pick_row = jnp.where(lane % cap < count_row, pick_row, -1)
    token_ids = lax.broadcasted_iota(jnp.int32, (n_tok, slots), 0)
    sel[...] = jnp.where(token_ids == pick_row, 1.0, 0.0).astype(BF)

    load_tok.wait()
    send_f[...] = dot(sel[...], tok[...], TN).astype(BF).reshape(send_f.shape)

    pl.semaphore_wait(barrier, shards - 1 + parts - 1)

    w = Wires(send_sems, recv_sems)

    def exchange(src_at, recv):
        base = w.take(shards)

        for dz, dy in OFFSETS:
            to = wrap(z + dz) * RING + wrap(y + dy)
            w.send(base + dz * RING + dy, src_at(to), recv.at[s], (to, t), keep=False)
        recv[s] = src_at(s)[...]
        return base

    def exchanged(base, recv):
        for dz, dy in OFFSETS:
            source = wrap(z - dz) * RING + wrap(y - dy)
            w.arrived(base + dz * RING + dy, recv.at[source], (source, t))

    def exchange_end(base, recv):
        def body(i, carry):
            w.copy(base + i, recv.at[0], recv.at[0], to_sib).wait_send()
            return carry

        lax.fori_loop(1, shards, body, 0)

    class RowGather:
        def __init__(self, buf, first, count):
            self.buf = buf
            self.whole = lambda block: buf.at[block, pl.ds(first, count), :]

            def at(block, half):
                return buf.at[block, pl.ds(first + half * count // 2, count // 2), :]

            self.ring = RingGather(w, at, t, left, right, far, to_left, to_right)
            self.base = w.take(7)
            self.at = at

        def give(self, k, ref):
            w.send(self.base + k, ref, ref, to_sib)

        def start(self):
            self.ring.start(1)
            self.ring.start(0)
            self.give(0, self.whole(t))

        def forward(self):
            self.ring.forward(1)
            self.ring.forward(0)
            self.give(1, self.at(left, 1))
            self.give(2, self.at(right, 0))

        def near(self):
            self.ring.near(0)
            self.ring.near(1)
            self.give(3, self.at(left, 0))
            self.give(4, self.at(right, 1))

        def last(self):
            self.ring.last(1)
            self.ring.last(0)
            self.give(5, self.at(far, 1))
            self.give(6, self.at(far, 0))

        def sib_own(self):
            w.arrived(self.base, self.whole(sib), to_sib)

        def sib_near(self):
            other = 1 - 2 * c
            for k, (block, half) in enumerate(((left, 1), (right, 0), (left, 0), (right, 1))):
                w.arrived(self.base + 1 + k, self.at(block + other, half), to_sib)

        def sib_last(self):
            other = 1 - 2 * c
            w.arrived(self.base + 5, self.at(far + other, 1), to_sib)
            w.arrived(self.base + 6, self.at(far + other, 0), to_sib)

    ex_f = exchange(lambda to: send_f.at[to // 2], recv_f)
    part_rows = (5 * width // 16, 6 * width // 16, 5 * width // 16)
    qkv_rows = [RowGather(wq, sum(part_rows[:k]), n) for k, n in enumerate(part_rows)]
    load_qkv.wait()
    blocks = wq.shape[2] // 128
    turn = row_permutation(blocks, True)
    for f in range(0, width, BAND):
        moved = dot(turn, wraw[f * blocks:(f + BAND) * blocks, :]).astype(BF)
        for k in range(blocks):
            wq[t, f:f + BAND, k * 128:(k + 1) * 128] = moved[k * BAND:(k + 1) * BAND]

    qkv_rows[0].start()

    eye = (
        lax.broadcasted_iota(jnp.int32, (cap, cap), 0)
        == lax.broadcasted_iota(jnp.int32, (cap, cap), 1)
    )
    turned = lax.dot_general(
        jnp.where(eye, 1.0, 0.0).astype(F32), combine[...], NT,
        precision=lax.Precision.HIGHEST, preferred_element_type=F32,
    )
    for e in range(experts):
        wcol[e * cap:(e + 1) * cap, :] = turned[:, e:e + 1]

    padded = shards * cap
    lane = lax.broadcasted_iota(jnp.int32, (1, padded), 1)
    mine = s // 2
    offset = jnp.int32(0)
    offset_row = jnp.zeros((1, padded), jnp.int32)
    count_row = jnp.zeros((1, padded), jnp.int32)
    for shard in range(shards):
        count = counts[mine, shard]
        here = lane // cap == shard
        offset_row = jnp.where(here, offset, offset_row)
        count_row = jnp.where(here, count, count_row)
        offset = offset + count
    position = jnp.where(lane % cap < count_row, offset_row + lane % cap, -1)
    row_ids = lax.broadcasted_iota(jnp.int32, comp.shape, 0)
    comp[...] = jnp.where(row_ids == position, 1.0, 0.0).astype(BF)

    load_half.wait()
    for k in range(RING):
        part = slice(k * width, (k + 1) * width)
        taken = dot(sel[...], ups_half[:, part], TN) * wcol[...]
        send_b[:, :, part] = taken.astype(BF).reshape(experts, cap, width)

    other = 1 - 2 * c

    def win_at(j):
        return win[pl.ds(pl.multiple_of(j * width, width), width), :]

    def wout_at(j):
        return wout[:, pl.ds(pl.multiple_of(j * width, width), width)]

    def gathered(gather, weight_at, dims):
        buf = gather.buf

        def add(j, first=False):
            term = dot(buf[j], weight_at(j), dims)
            if first:
                acc[...] = term
            else:
                acc[...] += term

        add(t, True)
        gather.sib_own()
        add(sib)
        gather.near()
        add(left)
        add(right)
        gather.last()
        gather.sib_near()
        add(left + other)
        add(right + other)
        add(far)
        gather.sib_last()
        add(far + other)

    class RowReduce:
        def __init__(self, k):
            self.k = k
            self.base = w.take(10)

        def partials(self, lhs, weight_at, dims):
            k, b = self.k, self.base
            for d in (2, 1, 3, 0):
                j = wrap(x + d) * 2 + 1 - c
                pst[k, d] = dot(lhs[...], weight_at(j), dims).astype(BF)
                w.send(b + d, pst.at[k, d], d2d.at[k, d], to_sib)
            lo, hi = pl.ds(0, half_rows), pl.ds(half_rows, half_rows)
            for d in (2, 1, 3, 0):
                j = wrap(x + d) * 2 + c
                own = dot(lhs[...], weight_at(j), dims)
                w.arrived(b + d, d2d.at[k, d], to_sib)
                sbuf[k, d] = (own + d2d[k, d].astype(F32)).astype(BF)
                if d == 2:
                    w.send(b + 4, sbuf.at[k, d, hi], half_l.at[k], to_right)
                    w.send(b + 5, sbuf.at[k, d, lo], half_r.at[k], to_left)
                elif d == 1:
                    w.send(b + 6, sbuf.at[k, d, lo], full_l.at[k, lo], to_right)
                elif d == 3:
                    w.send(b + 7, sbuf.at[k, d, hi], full_r.at[k, hi], to_left)

        def forward(self):
            k, b = self.k, self.base
            lo, hi = pl.ds(0, half_rows), pl.ds(half_rows, half_rows)
            w.arrived(b + 4, half_l.at[k], to_right)
            sbuf[k, 1, hi] = (sbuf[k, 1, hi].astype(F32) + half_l[k].astype(F32)).astype(BF)
            w.send(b + 8, sbuf.at[k, 1, hi], full_l.at[k, hi], to_right)
            w.arrived(b + 5, half_r.at[k], to_left)
            sbuf[k, 3, lo] = (sbuf[k, 3, lo].astype(F32) + half_r[k].astype(F32)).astype(BF)
            w.send(b + 9, sbuf.at[k, 3, lo], full_r.at[k, lo], to_left)

        def result(self):
            k, b = self.k, self.base
            lo, hi = pl.ds(0, half_rows), pl.ds(half_rows, half_rows)
            w.arrived(b + 6, full_l.at[k, lo], to_right)
            w.arrived(b + 7, full_r.at[k, hi], to_left)
            w.arrived(b + 8, full_l.at[k, hi], to_right)
            w.arrived(b + 9, full_r.at[k, lo], to_left)
            total = sbuf[k, 0].astype(F32) + full_l[k].astype(F32) + full_r[k].astype(F32)
            return total.astype(BF)

    def send_back(k, rows):
        ret_s[k] = dot(comp[...], rows, TN).astype(BF).reshape(ret_s.shape[1:])
        return exchange(lambda to: ret_s.at[k, to], ret_r.at[k])

    def returned(k, base):
        exchanged(base, ret_r.at[k])
        pairs = ret_r[k].reshape(experts, 2, cap, width).astype(F32)
        return (pairs[:, 0] + pairs[:, 1]).reshape(slots, width)

    def scatter(values):
        high = values.astype(BF)
        low = (values - high.astype(F32)).astype(BF)
        return dot(sel[...], high) + dot(sel[...], low)

    gather_f = RowGather(ag_f, 0, n_tok)
    exchanged(ex_f, recv_f)
    ag_f[t] = dot(comp[...], recv_f[...].reshape(padded, width)).astype(BF)
    gather_f.start()
    ex_b = exchange(lambda to: send_b.at[to // 2], recv_b)
    gather_f.forward()
    qkv_rows[0].forward()
    load_win.wait()
    gathered(gather_f, win_at, NN)
    pre = acc[...]
    cdf = 0.5 * (1.0 + lax.erf(pre * 0.7071067811865476))
    hid[...] = (pre * cdf).astype(BF)
    slope[...] = cdf + pre * jnp.exp(-0.5 * pre * pre) * 0.3989422804014327
    load_wout.wait()
    reduce_f = RowReduce(0)
    reduce_f.partials(hid, wout_at, NN)


    reduce_f.forward()
    qkv_rows[0].near()
    qkv_rows[0].last()
    back_f = send_back(0, reduce_f.result())
    qkv_rows[1].start()

    give_b = w.take(RING)
    exchanged(ex_b, recv_b)
    for k in range(RING):
        part = recv_b[:, :, k * width:(k + 1) * width].reshape(padded, width)
        mine_k = ag_b.at[c * RING + k]
        mine_k[...] = dot(comp[...], part).astype(BF)
        w.send(give_b + k, mine_k, mine_k, to_sib)
    for k in range(2 * RING):
        j = c * RING + k if k < RING else (1 - c) * RING + k - RING
        if k >= RING:
            w.arrived(give_b + k - RING, ag_b.at[j], to_sib)
        term = dot(ag_b[j], wout_at(j), NT)
        if k == 0:
            acc[...] = term
        else:
            acc[...] += term
    pgr[...] = (acc[...] * slope[...]).astype(BF)
    halves = returned(0, back_f)
    mixture = scatter(halves * wcol[...])
    layer = (tok[...].astype(F32) + mixture).astype(BF)
    lay_s[...] = layer.reshape(lay_s.shape)
    line_base = w.take(parts)

    def line_end(i, carry):
        w.copy(line_base + i, lay_s.at[0], lay_s.at[0], to_sib).wait_send()
        return carry

    for to in (sib, far, far + other, left, left + other, right, right + other):
        slot = line_base + lax.rem(to - t + parts, parts)
        w.send(slot, lay_s.at[to], lay.at[z, y, t], (s, to), keep=False)
    lay[z, y, t] = lay_s[t]

    def from_chip(chip):
        for core in range(2):
            source = chip * 2 + core
            w.arrived(
                line_base + lax.rem(t - source + parts, parts), lay.at[z, y, source], (s, source)
            )

    chips = ((x, wrap(x + 2)), (wrap(x + 1), wrap(x - 1)))

    def along_y(part, zz):
        def at(pos, half):
            return lay.at[zz, pos, pl.ds(chips[part][half] * 2, 2)]
        return RingGather(w, at, y, y_minus, y_plus, y_far, to_ym, to_yp)

    def along_z(part, yy):
        def at(pos, half):
            return lay.at[pos, yy, pl.ds(chips[part][half] * 2, 2)]
        return RingGather(w, at, z, z_minus, z_plus, z_far, to_zm, to_zp)

    first_p, first_q = along_y(0, z), along_z(1, y)
    second_p = [along_z(0, yy) for yy in (y, y_minus, y_plus, y_far)]
    second_q = [along_y(1, zz) for zz in (z, z_minus, z_plus, z_far)]
    w.arrived(line_base + lax.rem(t - sib + parts, parts), lay.at[z, y, sib], to_sib)
    first_p.start(0)
    second_p[0].start(0)
    reduce_b = RowReduce(1)
    reduce_b.partials(pgr, win_at, NT)
    for half in (0, 1):
        from_chip(chips[1][half])
        first_q.start(half)
        second_q[0].start(half)
    from_chip(chips[0][1])
    first_p.start(1)
    second_p[0].start(1)

    rows_of_four = RING * piece

    def products(blocks_at, part):
        total = None
        for half in range(2):
            for core in range(2):
                k = chips[part][half] * 2 + core
                term = dot(blocks_at(k).reshape(rows_of_four, width), wq[k])
                total = term if total is None else total + term
        return total.reshape(RING, piece, -1)

    def group_p(zz):
        sum_p[zz] = products(lambda k: lay[zz, :, k], 0)

    def group_q(yy):
        sum_q[:, yy] = products(lambda k: lay[:, yy, k], 1)

    out_base = w.take(2 * parts)

    def out_copy(zz, yy):
        to = zz * 2 + yy // 2
        return to, pltpu.make_async_remote_copy(
            src_ref=out_s.at[zz, yy],
            dst_ref=projected.at[lax.rem(yy, 2), t],
            send_sem=send_sems.at[out_base + zz * RING + yy],
            recv_sem=recv_sems.at[out_base + lax.rem(yy, 2) * parts + t],
            device_id=(s, to),
            device_id_type=pl.DeviceIdType.MESH,
        )

    def deliver(zz, yy):
        out_s[zz, yy] = (sum_p[zz, yy] + sum_q[zz, yy]).astype(BF)
        to, copy = out_copy(zz, yy)

        @pl.when(to != t)
        def _():
            copy.start()

        @pl.when(to == t)
        def _():
            projected[lax.rem(yy, 2), t] = out_s[zz, yy]

    first_p.forward(0)
    second_p[0].forward(0)
    first_p.near(0)
    for k in (1, 2):
        second_p[k].start(0)
    qkv_rows[1].forward()
    qkv_rows[2].start()
    for half in (0, 1):
        first_q.forward(half)
        second_q[0].forward(half)
    for half in (0, 1):
        first_q.near(half)
        for k in (1, 2):
            second_q[k].start(half)
    first_p.forward(1)
    second_p[0].forward(1)
    first_p.near(1)
    first_p.last(0)
    for k in (1, 2):
        second_p[k].start(1)
    second_p[3].start(0)
    for k in (1, 2):
        second_p[k].forward(0)
    for half in (0, 1):
        first_q.last(half)
        second_q[3].start(half)
    first_p.last(1)
    second_p[3].start(1)
    reduce_b.forward()
    for k in (1, 2):
        for half in (0, 1):
            second_q[k].forward(half)
        second_p[k].forward(1)
    qkv_rows[2].forward()
    second_p[3].forward(0)
    for half in (0, 1):
        second_q[3].forward(half)
    second_p[3].forward(1)
    for gather in qkv_rows[1:]:
        gather.near()
        gather.last()
    for gather in qkv_rows:
        gather.sib_own()
        gather.sib_near()
        gather.sib_last()
    group_p(z)
    group_q(y)
    deliver(z, y)
    for k in range(RING):
        for half in (0, 1):
            second_p[k].near(half)
            second_q[k].near(half)
    group_p(z_plus)
    group_p(z_minus)
    deliver(z_plus, y)
    deliver(z_minus, y)
    group_q(y_plus)
    group_q(y_minus)
    for zz in (z_plus, z_minus, z):
        for yy in (y_plus, y_minus):
            deliver(zz, yy)
    back_b = send_back(1, reduce_b.result())
    for k in range(RING):
        second_p[k].last(0)
        second_p[k].last(1)
    group_p(z_far)
    for yy in (y_plus, y_minus, y):
        deliver(z_far, yy)
    for k in range(RING):
        second_q[k].last(0)
        second_q[k].last(1)
    group_q(y_far)
    for zz in (z_far, z_plus, z_minus, z):
        deliver(zz, y_far)

    hid_turned = hid[...].T
    for j in range(parts):
        part = slice(j * width, (j + 1) * width)
        grad_in[part, :] = dot(ag_f[j], pgr[...], TN).astype(BF)
        grad_out[:, part] = dot(hid_turned, ag_b[j]).astype(BF)
    load_ups.wait()
    back_rows = scatter(returned(1, back_b))
    grad_tokens[...] = (ups[...].astype(F32) + back_rows).astype(BF)

    def out_end(i, carry):
        to, copy = out_copy(i // RING, lax.rem(i, RING))

        @pl.when(to != t)
        def _():
            copy.wait_send()

        return carry

    def out_arrived(i, carry):
        source = lax.rem(t - i + parts, parts)
        for shard in range(2):
            slot = out_base + shard * parts + source
            w.arrived(slot, projected.at[shard, source], (s, source))
        return carry

    lax.fori_loop(1, parts, out_arrived, 0)
    lax.fori_loop(0, shards, out_end, 0)
    lax.fori_loop(1, parts, line_end, 0)

    for copy in w.sent:
        copy.wait_send()
    exchange_end(ex_f, recv_f)
    exchange_end(ex_b, recv_b)
    exchange_end(back_f, ret_r.at[0])
    exchange_end(back_b, ret_r.at[1])


def write_kernel(
    grad_in_v, grad_out_v, products, grads, projected, grad_tokens, grad_in, grad_out, turned, sems
):
    copies = []
    for src, dst in ((grad_in_v, grad_in.at[0]), (grad_out_v, grad_out.at[0]), (grads, grad_tokens)):
        copies.append(pltpu.make_async_copy(src, dst, sems.at[len(copies)]))
        copies[-1].start()
    blocks = products.shape[1] // 128
    turn = row_permutation(blocks, False)
    for f in range(0, products.shape[0], BAND):
        block = products[f:f + BAND, :]
        stacked = jnp.concatenate(
            [block[:, k * 128:(k + 1) * 128] for k in range(blocks)], axis=0
        )
        turned[f * blocks:(f + BAND) * blocks, :] = dot(turn, stacked).astype(BF)
    copies.append(pltpu.make_async_copy(turned, projected, sems.at[len(copies)]))
    copies[-1].start()
    for copy in copies:
        copy.wait()


def on_device(tokens, picked, counts, combine, w_in, w_out, w_qkv, upstream):
    n_tok, width = tokens.shape
    experts, cap = picked.shape[0], picked.shape[2]
    parts, shards = 8, 16
    slice_w = width // parts
    rows = experts * cap
    hidden = w_in.shape[2]
    heads, kinds, lanes = w_qkv.shape[1:]
    columns = heads * kinds * lanes
    flat = w_qkv.transpose(0, 2, 1, 3).reshape(slice_w * kinds * heads, lanes)
    anywhere = pl.BlockSpec(memory_space=pl.ANY)
    vmem = pl.BlockSpec(memory_space=pltpu.VMEM)
    smem = pl.BlockSpec(memory_space=pltpu.SMEM)
    sems = 340
    out = pl.pallas_call(
        layer_kernel,
        out_shape=(
            pltpu.VMEM((2, parts, n_tok // parts, columns), BF),
            pltpu.VMEM((n_tok, slice_w), BF),
            pltpu.VMEM((width, hidden), BF),
            pltpu.VMEM((hidden, width), BF),
        ),
        in_specs=[anywhere] * 5 + [vmem, smem, vmem],
        out_specs=[vmem] * 4,
        scratch_shapes=[
            pltpu.VMEM((n_tok, slice_w), BF),
            pltpu.VMEM((n_tok, slice_w), BF),
            pltpu.VMEM((n_tok, width // 2), BF),
            pltpu.VMEM((width, hidden), BF),
            pltpu.VMEM((hidden, width), BF),
            pltpu.VMEM(flat.shape, BF),
            pltpu.VMEM((parts, slice_w, columns), BF),
            pltpu.VMEM((n_tok, rows), BF),
            pltpu.VMEM((rows, shards * cap), BF),
            pltpu.VMEM((rows, 1), F32),
            pltpu.VMEM((experts, cap, slice_w), BF),
            pltpu.VMEM((experts, cap, width // 2), BF),
            pltpu.VMEM((shards, cap, slice_w), BF),
            pltpu.VMEM((shards, cap, width // 2), BF),
            pltpu.VMEM((parts, rows, slice_w), BF),
            pltpu.VMEM((parts, rows, slice_w), BF),
            pltpu.VMEM((rows, hidden), F32),
            pltpu.VMEM((rows, hidden), F32),
            pltpu.VMEM((rows, hidden), BF),
            pltpu.VMEM((rows, hidden), BF),
            pltpu.VMEM((2, RING, rows, slice_w), BF),
            pltpu.VMEM((2, RING, rows, slice_w), BF),
            pltpu.VMEM((2, RING, rows, slice_w), BF),
            pltpu.VMEM((2, rows // 2, slice_w), BF),
            pltpu.VMEM((2, rows // 2, slice_w), BF),
            pltpu.VMEM((2, rows, slice_w), BF),
            pltpu.VMEM((2, rows, slice_w), BF),
            pltpu.VMEM((2, shards, cap, slice_w), BF),
            pltpu.VMEM((2, shards, cap, slice_w), BF),
            pltpu.VMEM((parts, n_tok // parts, slice_w), BF),
            pltpu.VMEM((RING, RING, parts, n_tok // parts, slice_w), BF),
            pltpu.VMEM((RING, RING, n_tok // parts, columns), F32),
            pltpu.VMEM((RING, RING, n_tok // parts, columns), F32),
            pltpu.VMEM((RING, RING, n_tok // parts, columns), BF),
            pltpu.SemaphoreType.DMA((6,)),
            pltpu.SemaphoreType.DMA((sems,)),
            pltpu.SemaphoreType.DMA((sems,)),
        ],
        compiler_params=pltpu.CompilerParams(
            collective_id=0, has_side_effects=True, vmem_limit_bytes=50 * 1024 * 1024
        ),
        cost_estimate=pl.CostEstimate(
            flops=8 * 10**9, bytes_accessed=20 * 10**6, transcendentals=3 * 10**5
        ),
        name="moe_layer",
    )(
        tokens, upstream, w_in, w_out, flat,
        picked[:, 0, :], counts, combine[:, 0, :],
    )
    products, grads, grad_in, grad_out = out
    projected, grad_tokens, grad_in, grad_out = pl.pallas_call(
        write_kernel,
        out_shape=(
            jax.ShapeDtypeStruct((2 * n_tok * kinds * heads, lanes), BF),
            jax.ShapeDtypeStruct((n_tok, slice_w), BF),
            jax.ShapeDtypeStruct(w_in.shape, BF),
            jax.ShapeDtypeStruct(w_out.shape, BF),
        ),
        in_specs=[vmem] * 4,
        out_specs=(anywhere, anywhere, anywhere, anywhere),
        scratch_shapes=[
            pltpu.VMEM((2 * n_tok * kinds * heads, lanes), BF),
            pltpu.SemaphoreType.DMA((4,)),
        ],
        compiler_params=pltpu.CompilerParams(vmem_limit_bytes=16 * 1024 * 1024),
        cost_estimate=pl.CostEstimate(
            flops=2 * 10**8, bytes_accessed=18 * 10**6, transcendentals=0
        ),
        name="write_out",
    )(grad_in, grad_out, products.reshape(2 * n_tok, columns), grads)
    projected = projected.reshape(2 * n_tok, kinds, heads, lanes).transpose(0, 2, 1, 3)
    return projected, grad_tokens, grad_in, grad_out


def solution(mesh):
    return jax.shard_map(
        on_device,
        mesh=mesh,
        in_specs=(
            P("expert", None),
            P(None, "expert", None),
            P(),
            P(None, "expert", None),
            P("expert", None, "tensor"),
            P("expert", "tensor", None),
            P("tensor", "expert", None, None),
            P("expert", None),
        ),
        out_specs=(
            P("tensor", "expert", None, None),
            P("expert", "tensor"),
            P("expert", None, "tensor"),
            P("expert", "tensor", None),
        ),
        check_vma=False,
    )
```
